512 devices in a mesh: seq: 64 (over y, z_lo, core), head: 8 (over z_hi, x).
Axes of the slice: x: 4, y: 8, z: 8 (z_hi: 2, z_lo: 4; z = z_hi * 4 + z_lo), core: 2. Of those that a mesh axis runs over, the one named last changes fastest.
Arguments:
- frames: bfloat16 [8192, 1024], P('seq', 'head'), may hold values from -11 to 11
- weights: bfloat16 [3, 512, 1024], P(None, 'head')
- offset_table: bfloat16 [4096, 512], P('seq', 'head'), may hold values from -6 to 6
- clip_range: int32 [8], P('head'), may hold values from 1024 to 2047, as said below
- valid_frames: int32 [64], replicated, may hold values from 32 to 128, as said below
- context_grad: bfloat16 [8192, 512], P('seq', 'head'), may hold values from -192 to 192
Outputs:
- input_grad: bfloat16 [8192, 1024], P('seq', 'head')
- table_grad: float32 [4096, 512], P('seq', 'head')
The draws below stay inside these ranges and needn't reach their ends.
Inputs may be any that keep to these rules, and one draw needn't show every extreme that they name: `clip_range`: each head's clip lies inside the table's offsets; some head has the largest clip. `valid_frames`: frames of a block at or past its entry are padding and are never attended to; some block is full and some holds the fewest.
All inputs are finite; a program needn't handle non-finite values.
Results may differ from the reference program's by a relative error of at most 0.03.
Values may be sent and summed in bfloat16 or wider, within the bound.
No kernel may reach another device: no remote copies, remote signals or barrier semaphores. Data moves between devices by JAX's collectives and lax.ppermute only.
A program may use at most 64 MiB of HBM per device.

```python
import math
import jax
import jax.numpy as jnp
from jax import lax

D = 1024
HEAD_DIM = 64
TOK_DEV = 128
FRAMES = 8192
TABLE = 4096
HEADS = 8
BLOCKS = 64


def draw_frames(key, part):
    key = jax.random.fold_in(key, 11)
    values = jnp.clip(jax.random.normal(key, (FRAMES, D), jnp.float32), -4.0, 4.0)
    return values.astype(jnp.bfloat16)


def draw_weights(key, part):
    key = jax.random.fold_in(key, 12)
    shape = (3, HEADS * HEAD_DIM, D)
    mixed = jnp.clip(jax.random.normal(key, shape, jnp.float32), -6.0, 6.0)
    return (mixed * D ** (-0.5)).astype(jnp.bfloat16)


def draw_clip_range(key, part):
    key = jax.random.fold_in(key, 13)
    reach = jax.random.randint(key, (HEADS,), FRAMES // 8, FRAMES // 4)
    order = jax.random.permutation(jax.random.fold_in(key, 1), HEADS)
    reach = reach.at[order[0]].set(FRAMES // 4 - 1)
    if HEADS >= 3:
        reach = reach.at[order[1]].set(FRAMES // 8)
    return reach.astype(jnp.int32)


def draw_valid_frames(key, part):
    key = jax.random.fold_in(key, 14)
    counts = jax.random.randint(key, (BLOCKS,), TOK_DEV // 4, TOK_DEV + 1)
    order = jax.random.permutation(jax.random.fold_in(key, 1), BLOCKS)
    counts = counts.at[order[0]].set(TOK_DEV).at[order[1]].set(TOK_DEV // 4)
    return counts.astype(jnp.int32)


def level_of(own_key, shape, pieces, smallest, high):
    level = 1.0
    for axis_at, parts in pieces:
        heights = jax.random.uniform(jax.random.fold_in(jax.random.fold_in(own_key, 6), axis_at), (parts,), jnp.float32, smallest / len(pieces), high / len(pieces))
        level = level * jnp.repeat(jnp.exp(heights), shape[axis_at] // parts).reshape((-1,) + (1,) * (len(shape) - 1 - axis_at))
    return level


def gaussian(stream_key, extent, deviation, limit, cuts=(), kind=jnp.bfloat16):
    loudness = level_of(stream_key, extent, cuts, -0.22, 0.18) if cuts else 1.0
    array = jax.random.normal(stream_key, extent, jnp.float32) * deviation * loudness
    return jnp.minimum(jnp.maximum(array, -limit), limit).astype(kind)


def setup_inputs(seed: int = 0) -> dict:
    key_list = jax.random.split(jax.random.key(seed), 7)
    return {
        "frames": draw_frames(jax.random.fold_in(key_list[6], 71), 0),
        "weights": draw_weights(jax.random.fold_in(key_list[6], 71), 0),
        "offset_table": gaussian(key_list[2], (TABLE, HEADS * HEAD_DIM), 1.0, 6.0, ((0, 64), (1, 8))),
        "clip_range": draw_clip_range(jax.random.fold_in(key_list[6], 71), 0),
        "valid_frames": draw_valid_frames(jax.random.fold_in(key_list[6], 71), 0),
        "context_grad": gaussian(key_list[5], (FRAMES, HEADS * HEAD_DIM), 32.0, 192.0, ((0, 64), (1, 8))),
    }


def head_pass(frames, weights, offset_table, clip_range, context_grad, head_index, live_keys):
    score_scale = HEAD_DIM ** -0.5
    middle = TABLE // 2
    block_rows = math.gcd(FRAMES, 512)
    w_head = lax.dynamic_slice_in_dim(weights, head_index * HEAD_DIM, HEAD_DIM, 1)
    projected = [jnp.dot(frames, w_head[part_index].T, preferred_element_type=jnp.float32).astype(jnp.bfloat16) for part_index in range(3)]
    queries, key_rows, values = projected
    tab_head = lax.dynamic_slice_in_dim(offset_table, head_index * HEAD_DIM, HEAD_DIM, 1)
    upstream = lax.dynamic_slice_in_dim(context_grad, head_index * HEAD_DIM, HEAD_DIM, 1)
    clip_reach = clip_range[head_index]
    key_places = jnp.arange(FRAMES, dtype=jnp.int32)
    table_shift = jnp.arange(TABLE, dtype=jnp.int32) - middle

    def one_block(running, block_index):
        d_keys, d_values, d_table = running
        first_row = block_index * block_rows
        query_block = lax.dynamic_slice_in_dim(queries, first_row, block_rows, 0)
        grad_block = lax.dynamic_slice_in_dim(upstream, first_row, block_rows, 0)
        query_places = first_row + jnp.arange(block_rows, dtype=jnp.int32)
        relative = key_places[None, :] - query_places[:, None]
        content = jnp.dot(query_block, key_rows.T, preferred_element_type=jnp.float32)
        against = jnp.dot(query_block, tab_head.T, preferred_element_type=jnp.float32)
        lookup = jnp.clip(relative, -clip_reach, clip_reach) + middle
        positional = jnp.take_along_axis(against, lookup, axis=1)
        scores = jnp.where(live_keys[None, :], score_scale * (content + positional), -jnp.inf)
        row_max = jnp.max(scores, axis=1, keepdims=True)
        log_total = row_max + jnp.log(jnp.sum(jnp.exp(scores - row_max), axis=1, keepdims=True))
        attention = jnp.exp(scores - log_total)
        slope_term = jnp.dot(grad_block, values.T, preferred_element_type=jnp.float32)
        mean_slope = jnp.sum(attention * slope_term, axis=1, keepdims=True)
        score_grads = (attention * (slope_term - mean_slope)).astype(jnp.bfloat16)
        attention_low = attention.astype(jnp.bfloat16)
        grads_wide = score_grads.astype(jnp.float32)
        column = query_places[:, None] + table_shift[None, :]
        inside = (jnp.abs(table_shift)[None, :] < clip_reach) & (column >= 0) & (column < FRAMES)
        picked = jnp.take_along_axis(grads_wide, jnp.clip(column, 0, FRAMES - 1), axis=1)
        upper_tail = jnp.sum(jnp.where(relative >= clip_reach, grads_wide, 0.0), axis=1, keepdims=True)
        lower_tail = jnp.sum(jnp.where(relative <= -clip_reach, grads_wide, 0.0), axis=1, keepdims=True)
        d_against = jnp.where(inside, picked, 0.0)
        d_against = d_against + jnp.where(table_shift[None, :] == clip_reach, upper_tail, 0.0)
        d_against = d_against + jnp.where(table_shift[None, :] == -clip_reach, lower_tail, 0.0)
        d_query = score_scale * (jnp.dot(score_grads, key_rows, preferred_element_type=jnp.float32) + jnp.dot(d_against, tab_head.astype(jnp.float32), precision=lax.Precision.HIGHEST))
        d_keys = d_keys + score_scale * jnp.dot(score_grads.T, query_block, preferred_element_type=jnp.float32)
        d_values = d_values + jnp.dot(attention_low.T, grad_block, preferred_element_type=jnp.float32)
        d_table = d_table + score_scale * jnp.dot(d_against.T, query_block.astype(jnp.float32), precision=lax.Precision.HIGHEST)
        return (d_keys, d_values, d_table), d_query

    zero_rows = jnp.zeros((FRAMES, HEAD_DIM), jnp.float32)
    start_state = (zero_rows, zero_rows, jnp.zeros((TABLE, HEAD_DIM), jnp.float32))
    (d_keys, d_values, d_table), d_query = lax.scan(one_block, start_state, jnp.arange(FRAMES // block_rows, dtype=jnp.int32))
    d_query = d_query.reshape(FRAMES, HEAD_DIM)
    stacked = jnp.concatenate([d_query, d_keys, d_values], axis=1).astype(jnp.bfloat16)
    input_part = jnp.dot(stacked, w_head.reshape(3 * HEAD_DIM, D), preferred_element_type=jnp.float32)
    return input_part, d_table


def reference(frames, weights, offset_table, clip_range, valid_frames, context_grad):
    key_places = jnp.arange(FRAMES, dtype=jnp.int32)
    live_keys = (key_places % TOK_DEV) < valid_frames[key_places // TOK_DEV]

    def one_head(running, head_index):
        input_part, d_table = head_pass(frames, weights, offset_table, clip_range, context_grad, head_index, live_keys)
        return running + input_part, d_table

    input_sum, table_parts = lax.scan(one_head, jnp.zeros((FRAMES, D), jnp.float32), jnp.arange(HEADS, dtype=jnp.int32))
    table_grad = jnp.transpose(table_parts, (1, 0, 2)).reshape(TABLE, HEADS * HEAD_DIM)
    return input_sum.astype(jnp.bfloat16), table_grad
```

```python
import jax
import jax.numpy as jnp
from jax import lax
from jax.experimental import pallas as pl
from jax.experimental.pallas import tpu as pltpu
from jax.sharding import Mesh
from jax.sharding import PartitionSpec as P

B = 128
G = 8
E = 64
N = B * G
TABLE = 4096
REACH = 17
PAD = 256
WIDE = TABLE + 2 * PAD
SCALE = E ** (-0.5)
STEP = 2
HIDDEN = -1e30
BF = jnp.bfloat16
F32 = jnp.float32
LIMIT = 48 * 1024 * 1024


def nt(a, b):
    return lax.dot_general(a, b, (((1,), (1,)), ((), ())), preferred_element_type=F32)


def nn(a, b):
    return lax.dot_general(a, b, (((1,), (0,)), ((), ())), preferred_element_type=F32)


def whole(shape):
    return pl.BlockSpec(shape, lambda *_: (0,) * len(shape))


def project_kernel(frames_ref, weights_ref, grad_ref, table_ref, near_ref, kv_ref):
    total = jnp.zeros((B, 3 * E), F32)
    for h in range(G):
        total = total + nt(frames_ref[h], weights_ref[:, h * B : (h + 1) * B])
    low = total.astype(BF)
    scaled = (low[:, :E].astype(F32) * SCALE).astype(BF)
    paired = jnp.concatenate([scaled, grad_ref[...]], axis=1)
    for g in range(G):
        near_ref[g, :B] = paired
        near_ref[g, B:] = table_ref[...]
    kv_ref[...] = low[:, E:]


def project(frames, weights, grad, table):
    return pl.pallas_call(
        project_kernel,
        out_shape=(
            jax.ShapeDtypeStruct((G, B + 32, B), BF),
            jax.ShapeDtypeStruct((B, B), BF),
        ),
        compiler_params=pltpu.CompilerParams(vmem_limit_bytes=LIMIT),
        name="project",
    )(frames, weights, grad, table)


def tile_start(place, u, v):
    apart = G * (v - place[0]) + place[1] - u
    return pl.multiple_of((jnp.clip(apart, -REACH, REACH) + REACH) * B, B)


def stats_kernel(place, valid, near_ref, far_ref, scores_ref, stats_ref, table_ref):
    step = pl.program_id(0)
    clip = place[2]

    @pl.when(step == 0)
    def _():
        table_ref[:, :PAD] = jnp.zeros((E, PAD), BF)
        table_ref[:, WIDE - PAD :] = jnp.zeros((E, PAD), BF)
        for y in range(G):
            for k in range(4):
                at = PAD + (4 * y + k) * B
                table_ref[:, at : at + B] = far_ref[y, B + k * E : B + (k + 1) * E, :]
        offsets = lax.broadcasted_iota(jnp.int32, (E, WIDE), 1) - (TABLE // 2 + PAD)
        rows = table_ref[...].astype(F32)
        upper = jnp.sum(jnp.where(offsets == clip, rows, 0.0), axis=1, keepdims=True)
        lower = jnp.sum(jnp.where(offsets == -clip, rows, 0.0), axis=1, keepdims=True)
        rows = jnp.where(offsets >= clip, upper, jnp.where(offsets <= -clip, lower, rows))
        table_ref[...] = rows.astype(BF)

    keys = far_ref[:, :B, :E].reshape(N, E)
    values = far_ref[:, :B, E:].reshape(N, E)
    lane = lax.broadcasted_iota(jnp.int32, (B, B), 1)
    for part in range(STEP):
        u = step * STEP + part
        queries = near_ref[u, :B, :E]
        grads = near_ref[u, :B, E:]
        content = nt(queries, keys)
        slope = nt(grads, values)
        pieces = []
        for v in range(G):
            band = nn(queries, table_ref[:, pl.ds(tile_start(place, u, v), 2 * B)])
            moved = pltpu.roll(band, B, 1, stride=1, stride_axis=0)[:, :B]
            live = lane < valid[G * v + place[1]]
            pieces.append(jnp.where(live, content[:, v * B : (v + 1) * B] + moved, HIDDEN))
        scores = jnp.concatenate(pieces, axis=1)
        scores_ref[part * B : (part + 1) * B, :] = scores
        top = jnp.max(scores, axis=1, keepdims=True)
        weight = jnp.exp(scores - top)
        amount = jnp.sum(weight, axis=1, keepdims=True)
        mean = jnp.sum(weight * slope, axis=1, keepdims=True) / amount
        both = jnp.where(lane == 0, top + jnp.log(amount), jnp.where(lane == 1, mean, 0.0))
        turned = both.T
        stats_ref[pl.ds(u, 1), :] = turned[0:1]
        stats_ref[pl.ds(G + u, 1), :] = turned[1:2]


def statistics(place, valid, near, far):
    return pl.pallas_call(
        stats_kernel,
        grid_spec=pltpu.PrefetchScalarGridSpec(
            num_scalar_prefetch=2,
            grid=(G // STEP,),
            in_specs=[whole(near.shape), whole(far.shape)],
            out_specs=[
                pl.BlockSpec((STEP * B, N), lambda i, *_: (i, 0)),
                whole((2 * G, B)),
                whole((E, WIDE)),
            ],
        ),
        out_shape=(
            jax.ShapeDtypeStruct((N, N), F32),
            jax.ShapeDtypeStruct((2 * G, B), F32),
            jax.ShapeDtypeStruct((E, WIDE), BF),
        ),
        compiler_params=pltpu.CompilerParams(vmem_limit_bytes=LIMIT),
        name="statistics",
    )(place, valid, near, far)


def grads_kernel(
    place,
    near_ref,
    far_ref,
    scores_ref,
    parts_ref,
    table_ref,
    far_out,
    near_out,
    columns,
    pair_sum,
    table_sum,
):
    step = pl.program_id(0)
    clip = place[2]

    @pl.when(step == 0)
    def _():
        parts = parts_ref[...]
        each = parts[:, :G]
        top = jnp.max(each, axis=0)
        total = top + jnp.log(jnp.sum(jnp.exp(each - top[None]), axis=0))
        mean = jnp.sum(jnp.exp(each - total[None]) * parts[:, G:], axis=0)
        rest = jnp.zeros((B - 2 * G, B), F32)
        columns[...] = jnp.concatenate([total, mean, rest], axis=0).T
        pair_sum[...] = jnp.zeros_like(pair_sum)
        table_sum[...] = jnp.zeros_like(table_sum)

    keys = far_ref[:, :B, :E].reshape(N, E)
    values = far_ref[:, :B, E:].reshape(N, E)
    row = lax.broadcasted_iota(jnp.int32, (B, B), 0)
    lane = lax.broadcasted_iota(jnp.int32, (B, B), 1)
    turn = (lane + row) % B
    early = lane + row < B
    lows, probs, turned = [], [], []
    for part in range(STEP):
        u = step * STEP + part
        paired = near_ref[u, :B, :]
        flipped = paired.astype(F32).T.astype(BF)
        turned.append(flipped)
        total = jnp.sum(jnp.where(lane == u, columns[...], 0.0), axis=1, keepdims=True)
        mean = jnp.sum(jnp.where(lane == G + u, columns[...], 0.0), axis=1, keepdims=True)
        slope = nt(paired[:, E:], values)
        prob = jnp.exp(scores_ref[part * B : (part + 1) * B, :] - total)
        low = (prob * (slope - mean)).astype(BF)
        query_grad = nn(low, keys)
        wide = low.astype(F32)
        for v in range(G):
            at = tile_start(place, u, v)
            spun = jnp.take_along_axis(wide[:, v * B : (v + 1) * B], turn, axis=1)
            band = jnp.concatenate(
                [jnp.where(early, 0.0, spun), jnp.where(early, spun, 0.0)], axis=1
            ).astype(BF)
            query_grad = query_grad + nt(band, table_ref[:, pl.ds(at, 2 * B)])
            table_sum[:, pl.ds(at, 2 * B)] += nn(flipped[:E], band)
        query_low = (query_grad * SCALE).astype(BF)
        near_out[u] = jnp.concatenate([query_low[:E], query_low[E:]], axis=1)
        lows.append(low)
        probs.append(prob.astype(BF))
    both = jnp.concatenate(turned, axis=1)
    pair_sum[:E] += nn(both[:E], jnp.concatenate(lows, axis=0))
    pair_sum[E:] += nn(both[E:], jnp.concatenate(probs, axis=0))

    @pl.when(step == pl.num_programs(0) - 1)
    def _():
        offsets = lax.broadcasted_iota(jnp.int32, (E, WIDE), 1) - (TABLE // 2 + PAD)
        terms = table_sum[...]
        upper = jnp.sum(jnp.where(offsets >= clip, terms, 0.0), axis=1, keepdims=True)
        lower = jnp.sum(jnp.where(offsets <= -clip, terms, 0.0), axis=1, keepdims=True)
        terms = jnp.where(jnp.abs(offsets) < clip, terms, 0.0)
        terms = jnp.where(offsets == clip, upper, jnp.where(offsets == -clip, lower, terms))
        folded = terms.astype(BF)
        for y in range(G):
            far_out[y, :B] = pair_sum[:, y * B : (y + 1) * B].T.astype(BF)
            for k in range(4):
                at = PAD + (4 * y + k) * B
                far_out[y, B + k * E : B + (k + 1) * E, :] = folded[:, at : at + B]


def gradients(place, near, far, scores, parts, table):
    return pl.pallas_call(
        grads_kernel,
        grid_spec=pltpu.PrefetchScalarGridSpec(
            num_scalar_prefetch=1,
            grid=(G // STEP,),
            in_specs=[
                whole(near.shape),
                whole(far.shape),
                pl.BlockSpec((STEP * B, N), lambda i, *_: (i, 0)),
                whole(parts.shape),
                whole(table.shape),
            ],
            out_specs=[whole((G, B + 4 * E, B)), whole((G, E, B))],
            scratch_shapes=[
                pltpu.VMEM((B, B), F32),
                pltpu.VMEM((B, N), F32),
                pltpu.VMEM((E, WIDE), F32),
            ],
        ),
        out_shape=(
            jax.ShapeDtypeStruct((G, B + 4 * E, B), BF),
            jax.ShapeDtypeStruct((G, E, B), BF),
        ),
        compiler_params=pltpu.CompilerParams(vmem_limit_bytes=LIMIT),
        name="gradients",
    )(place, near, far, scores, parts, table)


def fold_kernel(far_ref, near_ref, kv_ref, out_ref):
    total = jnp.sum(far_ref[...].astype(F32), axis=0)
    kv_ref[...] = total[:B].astype(BF)
    low = total[B:].astype(BF)
    for k in range(4):
        block = low[k * E : (k + 1) * E]
        top, end = block[: E // 2], block[E // 2 :]
        out_ref[2 * k, :E] = near_ref[2 * k]
        out_ref[2 * k, E:] = jnp.concatenate([top[:, :E], end[:, :E]], axis=1)
        out_ref[2 * k + 1, :E] = near_ref[2 * k + 1]
        out_ref[2 * k + 1, E:] = jnp.concatenate([top[:, E:], end[:, E:]], axis=1)


def fold(far, near):
    return pl.pallas_call(
        fold_kernel,
        out_shape=(
            jax.ShapeDtypeStruct((B, B), BF),
            jax.ShapeDtypeStruct((G, E + E // 2, B), BF),
        ),
        compiler_params=pltpu.CompilerParams(vmem_limit_bytes=LIMIT),
        name="fold",
    )(far, near)


def unproject_kernel(near_ref, kv_ref, weights_ref, out_ref, table_ref):
    total = jnp.sum(near_ref[...].astype(F32), axis=0)
    packed = total[:E].astype(BF)
    query = jnp.concatenate([packed[:, :E], packed[:, E:]], axis=0)
    terms = nn(query, weights_ref[:E]) + nn(kv_ref[...], weights_ref[E:])
    for h in range(G):
        out_ref[h] = terms[:, h * B : (h + 1) * B].astype(BF)
    table_ref[...] = total[E:]


def unproject(near, kv, weights):
    return pl.pallas_call(
        unproject_kernel,
        out_shape=(
            jax.ShapeDtypeStruct((G, B, B), BF),
            jax.ShapeDtypeStruct((E // 2, B), F32),
        ),
        compiler_params=pltpu.CompilerParams(vmem_limit_bytes=LIMIT),
        name="unproject",
    )(near, kv, weights)


def exchange(parts, axis):
    return lax.all_to_all(parts, axis, 0, 0, tiled=True)


def to_all(shard):
    return jnp.broadcast_to(shard[None], (G,) + shard.shape)


def shards(frames, weights, offset_table, clip_range, valid_frames, context_grad):
    weight_rows = weights.reshape(3 * E, G * B)
    place = jnp.stack([lax.axis_index("far"), lax.axis_index("near"), clip_range[0]])
    turned = offset_table.T
    packed = jnp.concatenate([turned[: E // 2], turned[E // 2 :]], axis=1)
    gathered = exchange(to_all(frames), "head")
    near, kv = project(gathered, weight_rows, context_grad, packed)
    near = exchange(near, "near")
    rows = near[:, B:].reshape(4, 2, E // 2, 2, E)
    rows = rows.transpose(0, 3, 2, 1, 4).reshape(4 * E, B)
    far = exchange(to_all(jnp.concatenate([kv, rows], axis=0)), "far")
    scores, stats, table = statistics(place, valid_frames, near, far)
    parts = exchange(to_all(stats), "near")
    far_grads, near_grads = gradients(place, near, far, scores, parts, table)
    kv_grad, near_grads = fold(exchange(far_grads, "far"), near_grads)
    terms, table_part = unproject(exchange(near_grads, "near"), kv_grad, weight_rows)
    table_grad = table_part.reshape(E // 2, 2, E).transpose(2, 1, 0).reshape(E, E)
    terms = exchange(terms, "head")
    input_grad = jnp.sum(terms.astype(F32), axis=0).astype(BF)
    return (input_grad, table_grad)


def solution(mesh):
    split = Mesh(mesh.devices.reshape(G, G, G), ("far", "near", "head"))
    seq = ("far", "near")
    placed = (
        P(seq, "head"),
        P(None, "head", None),
        P(seq, "head"),
        P("head"),
        P(),
        P(seq, "head"),
    )
    return jax.shard_map(
        shards,
        mesh=split,
        in_specs=placed,
        out_specs=(P(seq, "head"), P(seq, "head")),
        check_vma=False,
    )
```

```python
import jax
import jax.numpy as jnp
from jax import lax
from jax.experimental import pallas as pl
from jax.experimental.pallas import tpu as pltpu
from jax.sharding import Mesh
from jax.sharding import PartitionSpec as P

B = 128
G = 8
E = 64
N = B * G
TABLE = 4096
REACH = 17
PAD = 256
WIDE = TABLE + 2 * PAD
SCALE = E ** (-0.5)
SPAN = 2
STRIDES = (32, 16, 8, 4, 2)
HIDDEN = -1e30
BF = jnp.bfloat16
F32 = jnp.float32
LIMIT = 32 * 1024 * 1024


def nt(a, b):
    return lax.dot_general(a, b, (((1,), (1,)), ((), ())), preferred_element_type=F32)


def nn(a, b):
    return lax.dot_general(a, b, (((1,), (0,)), ((), ())), preferred_element_type=F32)


def project_kernel(frames_ref, weights_ref, grad_ref, near_ref, far_ref):
    total = jnp.zeros((B, 3 * E), F32)
    for h in range(G):
        total = total + nt(frames_ref[h], weights_ref[:, h * B : (h + 1) * B])
    low = total.astype(BF)
    scaled = (low[:, :E].astype(F32) * SCALE).astype(BF)
    paired = jnp.concatenate([scaled, grad_ref[...]], axis=1)
    for g in range(G):
        near_ref[g] = paired
        far_ref[g] = low[:, E:]


def project(frames, weights, grad):
    return pl.pallas_call(
        project_kernel,
        out_shape=(jax.ShapeDtypeStruct((G, B, B), BF), jax.ShapeDtypeStruct((G, B, B), BF)),
        compiler_params=pltpu.CompilerParams(vmem_limit_bytes=LIMIT),
        name="project",
    )(frames, weights, grad)


def slot_column(place, slot):
    bits = sum(((slot >> k) & 1) * (STRIDES[k] // 2) for k in range(len(STRIDES)))
    own = place[0] * (G // 2) + place[1] // 2
    return pl.multiple_of(PAD + jnp.bitwise_xor(own, bits) * B, B)


def near_tiles(place, u):
    shift = place[1] - u
    first = jnp.where(shift >= 0, -2, -1)
    return [(place[0] + first + w, G * (first + w) + shift) for w in range(4)]


def band_at(apart):
    return pl.ds(pl.multiple_of((apart + REACH) * B, B), 2 * B)


def block_at(v):
    return pl.ds(pl.multiple_of((v + SPAN) * B, B), B)


def stats_kernel(
    place, valid, near_ref, far_ref, mine_ref, theirs_ref, scores_ref, stats_ref, table_ref, shifts
):
    clip = place[2]
    table_ref[:, :PAD] = jnp.zeros((E, PAD), BF)
    table_ref[:, WIDE - PAD :] = jnp.zeros((E, PAD), BF)
    first = place[1] % 2 == 0
    for slot in range(2 ** len(STRIDES)):
        mine = mine_ref[slot].astype(F32)
        theirs = theirs_ref[slot].astype(F32)
        left = jnp.where(first, mine, theirs)
        right = jnp.where(first, theirs, mine)
        top = jnp.concatenate([left[:, :E], right[:, :E]], axis=1)
        end = jnp.concatenate([left[:, E:], right[:, E:]], axis=1)
        block = jnp.concatenate([top, end], axis=0)
        table_ref[:, pl.ds(slot_column(place, slot), B)] = block.astype(BF)
    offsets = lax.broadcasted_iota(jnp.int32, (E, WIDE), 1) - (TABLE // 2 + PAD)
    rows = table_ref[...].astype(F32)
    upper = jnp.sum(jnp.where(offsets == clip, rows, 0.0), axis=1, keepdims=True)
    lower = jnp.sum(jnp.where(offsets == -clip, rows, 0.0), axis=1, keepdims=True)
    rows = jnp.where(offsets >= clip, upper, jnp.where(offsets <= -clip, lower, rows))
    table_ref[...] = rows.astype(BF)

    keys = far_ref[:, :, :E].reshape(N, E)
    values = far_ref[:, :, E:].reshape(N, E)
    ends = jnp.concatenate([table_ref[:, :B], table_ref[:, WIDE - B :]], axis=1)
    lane = lax.broadcasted_iota(jnp.int32, (B, B), 1)
    row = lax.broadcasted_iota(jnp.int32, (B, B), 0)
    late = lane + row < B

    def put_band(u, v, apart):
        band = nn(near_ref[u, :, :E], table_ref[:, band_at(apart)])
        picked = jnp.where(late, band[:, B:], band[:, :B])
        shifts[u, :, block_at(v)] = pltpu.roll(picked, 0, 1, stride=1, stride_axis=0)

    for u in range(G):
        edges = nn(near_ref[u, :, :E], ends)
        for v in range(G):
            at = (v + SPAN) * B
            shifts[u, :, at : at + B] = jnp.where(v > place[0], edges[:, B:], edges[:, :B])
    put_band(place[1], place[0] + 2, 2 * G)
    for u in range(G):
        content = nt(near_ref[u, :, :E], keys)
        slope = nt(near_ref[u, :, E:], values)
        for v, apart in near_tiles(place, u):
            put_band(u, v, apart)
        pieces = []
        for v in range(G):
            at = (v + SPAN) * B
            both = content[:, v * B : (v + 1) * B] + shifts[u, :, at : at + B]
            pieces.append(jnp.where(lane < valid[G * v + place[1]], both, HIDDEN))
        scores = jnp.concatenate(pieces, axis=1)
        scores_ref[u * B : (u + 1) * B, :] = scores
        top = jnp.max(scores, axis=1, keepdims=True)
        weight = jnp.exp(scores - top)
        amount = jnp.sum(weight, axis=1, keepdims=True)
        mean = jnp.sum(weight * slope, axis=1, keepdims=True) / amount
        both = jnp.where(lane == 0, top + jnp.log(amount), jnp.where(lane == 1, mean, 0.0))
        turned = both.T
        stats_ref[u : u + 1, :] = turned[0:1]
        stats_ref[G + u : G + u + 1, :] = turned[1:2]


SCALARS = pl.BlockSpec(memory_space=pltpu.SMEM)
ARRAY = pl.BlockSpec(memory_space=pltpu.VMEM)


def statistics(place, valid, near, far, mine, theirs):
    return pl.pallas_call(
        stats_kernel,
        in_specs=[SCALARS] * 2 + [ARRAY] * 4,
        out_specs=[ARRAY] * 3,
        out_shape=(
            jax.ShapeDtypeStruct((N, N), F32),
            jax.ShapeDtypeStruct((2 * G, B), F32),
            jax.ShapeDtypeStruct((E, WIDE), BF),
        ),
        scratch_shapes=[pltpu.VMEM((G, B, N + 2 * SPAN * B), F32)],
        compiler_params=pltpu.CompilerParams(vmem_limit_bytes=LIMIT),
        name="statistics",
    )(place, valid, near, far, mine, theirs)


def grads_kernel(
    place,
    near_ref,
    far_ref,
    scores_ref,
    parts_ref,
    table_ref,
    far_out,
    near_out,
    keep_out,
    send_out,
    query_sum,
    table_sum,
    held,
):
    clip = place[2]
    parts = parts_ref[...]
    each = parts[:, :G]
    top = jnp.max(each, axis=0)
    total = top + jnp.log(jnp.sum(jnp.exp(each - top[None]), axis=0))
    mean = jnp.sum(jnp.exp(each - total[None]) * parts[:, G:], axis=0)
    rest = jnp.zeros((B - 2 * G, B), F32)
    columns = jnp.concatenate([total, mean, rest], axis=0).T
    table_sum[...] = jnp.zeros_like(table_sum)
    held[:, :, : SPAN * B] = jnp.zeros((G, B, SPAN * B), F32)
    held[:, :, SPAN * B + N :] = jnp.zeros((G, B, SPAN * B), F32)

    keys = far_ref[:, :, :E].reshape(N, E)
    values = far_ref[:, :, E:].reshape(N, E)
    low_end, high_end = table_ref[:, :B], table_ref[:, WIDE - B :]
    ends = jnp.concatenate([low_end, high_end, low_end, high_end], axis=1)
    row = lax.broadcasted_iota(jnp.int32, (B, B), 0)
    lane = lax.broadcasted_iota(jnp.int32, (B, B), 1)
    turn = (lane + row) % B
    early = lane + row < B
    lows, probs, turned = [], [], []
    end_sum = jnp.zeros((E, 4 * B), F32)

    def add_band(u, v, apart, flipped):
        spun = jnp.take_along_axis(held[u, :, block_at(v)], turn, axis=1)
        band = jnp.concatenate(
            [jnp.where(early, 0.0, spun), jnp.where(early, spun, 0.0)], axis=1
        ).astype(BF)
        table_sum[:, band_at(apart)] += nn(flipped[:E], band)
        return nt(band, table_ref[:, band_at(apart)])

    for u in range(G):
        paired = near_ref[u]
        flipped = paired.astype(F32).T.astype(BF)
        turned.append(flipped)
        total = columns[:, u : u + 1]
        mean = columns[:, G + u : G + u + 1]
        slope = nt(paired[:, E:], values)
        prob = jnp.exp(scores_ref[u * B : (u + 1) * B, :] - total)
        low = (prob * (slope - mean)).astype(BF)
        wide = low.astype(F32)
        held[u, :, SPAN * B : SPAN * B + N] = wide
        lower = jnp.zeros((B, B), F32)
        upper = jnp.zeros((B, B), F32)
        for v in range(G):
            apart = G * (v - place[0]) + place[1] - u
            piece = wide[:, v * B : (v + 1) * B]
            lower = lower + jnp.where(apart <= -REACH, piece, 0.0)
            upper = upper + jnp.where(apart >= REACH, piece, 0.0)
        outer = jnp.concatenate([lower, upper], axis=1)
        coarse = outer.astype(BF)
        fine = (outer - coarse.astype(F32)).astype(BF)
        outer = jnp.concatenate([coarse, fine], axis=1)
        end_sum = end_sum + nn(flipped[:E], outer)
        query_grad = nn(low, keys) + nt(outer, ends)
        for v, apart in near_tiles(place, u):
            query_grad = query_grad + add_band(u, v, apart, flipped)
        query_sum[u] = query_grad
        lows.append(low)
        probs.append(prob.astype(BF))
    flipped = near_ref[place[1]].astype(F32).T.astype(BF)
    query_sum[place[1]] += add_band(place[1], place[0] + 2, 2 * G, flipped)
    for u in range(G):
        query_low = (query_sum[u] * SCALE).astype(BF)
        near_out[u] = jnp.concatenate([query_low[:E], query_low[E:]], axis=1)
    both = jnp.concatenate(turned, axis=1)
    pairs = jnp.concatenate(
        [nn(both[:E], jnp.concatenate(lows, axis=0)), nn(both[E:], jnp.concatenate(probs, axis=0))],
        axis=0,
    )
    offsets = lax.broadcasted_iota(jnp.int32, (E, WIDE), 1) - (TABLE // 2 + PAD)
    terms = table_sum[...]
    tails = end_sum
    tails = tails[:, : 2 * B] + tails[:, 2 * B :]
    upper = jnp.sum(jnp.where(offsets >= clip, terms, 0.0), axis=1, keepdims=True)
    lower = jnp.sum(jnp.where(offsets <= -clip, terms, 0.0), axis=1, keepdims=True)
    upper = upper + jnp.sum(tails[:, B:], axis=1, keepdims=True)
    lower = lower + jnp.sum(tails[:, :B], axis=1, keepdims=True)
    table_sum[...] = jnp.where(offsets == clip, upper, jnp.where(offsets == -clip, lower, terms))
    first = place[1] % 2 == 0
    for slot in range(2 ** len(STRIDES)):
        block = table_sum[:, pl.ds(slot_column(place, slot), B)]
        at = lane[:E] + (slot_column(place, slot) - (TABLE // 2 + PAD))
        block = jnp.where(jnp.abs(at) <= clip, block, 0.0)
        top, end = block[: E // 2], block[E // 2 :]
        left = jnp.concatenate([top[:, :E], end[:, :E]], axis=1)
        right = jnp.concatenate([top[:, E:], end[:, E:]], axis=1)
        keep_out[slot] = jnp.where(first, left, right)
        send_out[slot] = jnp.where(first, right, left).astype(BF)
    for y in range(G):
        far_out[y] = pairs[:, y * B : (y + 1) * B].T.astype(BF)


def gradients(place, near, far, scores, parts, table):
    return pl.pallas_call(
        grads_kernel,
        in_specs=[SCALARS] + [ARRAY] * 5,
        out_specs=[ARRAY] * 4,
        out_shape=(
            jax.ShapeDtypeStruct((G, B, B), BF),
            jax.ShapeDtypeStruct((G, E, B), BF),
            jax.ShapeDtypeStruct((32, E // 2, B), F32),
            jax.ShapeDtypeStruct((32, E // 2, B), BF),
        ),
        scratch_shapes=[
            pltpu.VMEM((G, B, E), F32),
            pltpu.VMEM((E, WIDE), F32),
            pltpu.VMEM((G, B, N + 2 * SPAN * B), F32),
        ],
        compiler_params=pltpu.CompilerParams(vmem_limit_bytes=LIMIT),
        name="gradients",
    )(place, near, far, scores, parts, table)


def unproject_kernel(far_ref, near_ref, weights_ref, out_ref):
    pairs = jnp.sum(far_ref[...].astype(F32), axis=0).astype(BF)
    packed = jnp.sum(near_ref[...].astype(F32), axis=0).astype(BF)
    query = jnp.concatenate([packed[:, :E], packed[:, E:]], axis=0)
    terms = nn(query, weights_ref[:E]) + nn(pairs, weights_ref[E:])
    for h in range(G):
        out_ref[h] = terms[:, h * B : (h + 1) * B].astype(BF)


def unproject(far, near, weights):
    return pl.pallas_call(
        unproject_kernel,
        out_shape=jax.ShapeDtypeStruct((G, B, B), BF),
        compiler_params=pltpu.CompilerParams(vmem_limit_bytes=LIMIT),
        name="unproject",
    )(far, near, weights)


def exchange(parts, axis):
    return lax.all_to_all(parts, axis, 0, 0, tiled=True)


def to_all(shard):
    return jnp.broadcast_to(shard[None], (G,) + shard.shape)


def across(shard, stride):
    return lax.ppermute(shard, ("far", "near"), [(i, i ^ stride) for i in range(G * G)])


def shards(frames, weights, offset_table, clip_range, valid_frames, context_grad):
    weight_rows = weights.reshape(3 * E, G * B)
    place = jnp.stack([lax.axis_index("far"), lax.axis_index("near"), clip_range[0]])
    turned = offset_table.T
    mine = jnp.concatenate([turned[: E // 2], turned[E // 2 :]], axis=1)[None]
    for stride in STRIDES:
        mine = jnp.concatenate([mine, across(mine, stride)], axis=0)
    theirs = across(mine, 1)
    gathered = exchange(to_all(frames), "head")
    near, far = project(gathered, weight_rows, context_grad)
    near = exchange(near, "near")
    far = exchange(far, "far")
    scores, stats, table = statistics(place, valid_frames, near, far, mine, theirs)
    parts = exchange(to_all(stats), "near")
    far, near, keep, send = gradients(place, near, far, scores, parts, table)
    total = keep + across(send, 1).astype(F32)
    for stride in reversed(STRIDES):
        half = total.shape[0] // 2
        arrived = across(total[half:].astype(BF), stride)
        total = total[:half] + arrived.astype(F32)
    terms = unproject(exchange(far, "far"), exchange(near, "near"), weight_rows)
    table_grad = total[0].reshape(E // 2, 2, E).transpose(2, 1, 0).reshape(E, E)
    terms = exchange(terms, "head")
    input_grad = jnp.sum(terms.astype(F32), axis=0).astype(BF)
    return (input_grad, table_grad)


def solution(mesh):
    split = Mesh(mesh.devices.reshape(G, G, G), ("far", "near", "head"))
    seq = ("far", "near")
    placed = (
        P(seq, "head"),
        P(None, "head", None),
        P(seq, "head"),
        P("head"),
        P(),
        P(seq, "head"),
    )
    return jax.shard_map(
        shards,
        mesh=split,
        in_specs=placed,
        out_specs=(P(seq, "head"), P(seq, "head")),
        check_vma=False,
    )
```

```python
import jax
import jax.numpy as jnp
from jax import lax
from jax.experimental import pallas as pl
from jax.experimental.pallas import tpu as pltpu
from jax.sharding import Mesh
from jax.sharding import PartitionSpec as P

B = 128
G = 8
E = 64
N = B * G
TABLE = 4096
REACH = 17
PAD = 256
WIDE = TABLE + 2 * PAD
SCALE = E ** (-0.5)
SPAN = 2
STRIDES = (4, 2)
SLOTS = 32
ROWS = B + E // 2
HIDDEN = -1e30
BF = jnp.bfloat16
F32 = jnp.float32
LIMIT = 32 * 1024 * 1024


def nt(a, b):
    return lax.dot_general(a, b, (((1,), (1,)), ((), ())), preferred_element_type=F32)


def nn(a, b):
    return lax.dot_general(a, b, (((1,), (0,)), ((), ())), preferred_element_type=F32)


def project_kernel(frames_ref, weights_ref, grad_ref, chunk_ref, near_ref, far_ref):
    total = jnp.zeros((B, 3 * E), F32)
    for h in range(G):
        total = total + nt(frames_ref[h], weights_ref[:, h * B : (h + 1) * B])
    low = total.astype(BF)
    scaled = (low[:, :E].astype(F32) * SCALE).astype(BF)
    paired = jnp.concatenate([scaled, grad_ref[...]], axis=1)
    for g in range(G):
        near_ref[g] = paired
        far_ref[g, :B] = low[:, E:]
        far_ref[g, B:] = chunk_ref[...]


def project(frames, weights, grad, chunk):
    return pl.pallas_call(
        project_kernel,
        out_shape=(jax.ShapeDtypeStruct((G, B, B), BF), jax.ShapeDtypeStruct((G, ROWS, B), BF)),
        compiler_params=pltpu.CompilerParams(vmem_limit_bytes=LIMIT),
        name="project",
    )(frames, weights, grad, chunk)


def slot_column(place, slot):
    turn, y = slot // G, slot % G
    block = 4 * y + jnp.bitwise_xor(place[1] // 2, (turn % 2) * 2 + turn // 2)
    return pl.multiple_of(PAD + block * B, B)


def near_tiles(place, u):
    shift = place[1] - u
    first = jnp.where(shift >= 0, -2, -1)
    return [(place[0] + first + w, G * (first + w) + shift) for w in range(4)]


def band_at(apart):
    return pl.ds(pl.multiple_of((apart + REACH) * B, B), 2 * B)


def block_at(v):
    return pl.ds(pl.multiple_of((v + SPAN) * B, B), B)


def stats_kernel(
    place,
    valid,
    near_ref,
    far_ref,
    mine_ref,
    theirs_ref,
    weight_ref,
    stats_ref,
    tops_ref,
    table_ref,
    shifts,
):
    clip = place[2]
    table_ref[:, :PAD] = jnp.zeros((E, PAD), BF)
    table_ref[:, WIDE - PAD :] = jnp.zeros((E, PAD), BF)
    first = place[1] % 2 == 0
    for slot in range(SLOTS):
        mine = mine_ref[slot].astype(F32)
        theirs = theirs_ref[slot].astype(F32)
        left = jnp.where(first, mine, theirs)
        right = jnp.where(first, theirs, mine)
        top = jnp.concatenate([left[:, :E], right[:, :E]], axis=1)
        end = jnp.concatenate([left[:, E:], right[:, E:]], axis=1)
        block = jnp.concatenate([top, end], axis=0)
        table_ref[:, pl.ds(slot_column(place, slot), B)] = block.astype(BF)
    offsets = lax.broadcasted_iota(jnp.int32, (E, WIDE), 1) - (TABLE // 2 + PAD)
    rows = table_ref[...].astype(F32)
    upper = jnp.sum(jnp.where(offsets == clip, rows, 0.0), axis=1, keepdims=True)
    lower = jnp.sum(jnp.where(offsets == -clip, rows, 0.0), axis=1, keepdims=True)
    rows = jnp.where(offsets >= clip, upper, jnp.where(offsets <= -clip, lower, rows))
    table_ref[...] = rows.astype(BF)

    keys = far_ref[:, :B, :E].reshape(N, E)
    values = far_ref[:, :B, E:].reshape(N, E)
    ends = jnp.concatenate([table_ref[:, :B], table_ref[:, WIDE - B :]], axis=1)
    lane = lax.broadcasted_iota(jnp.int32, (B, B), 1)
    row = lax.broadcasted_iota(jnp.int32, (B, B), 0)
    late = lane + row < B

    def put_band(u, v, apart):
        band = nn(near_ref[u, :, :E], table_ref[:, band_at(apart)])
        picked = jnp.where(late, band[:, B:], band[:, :B])
        shifts[u, :, block_at(v)] = pltpu.roll(picked, 0, 1, stride=1, stride_axis=0)

    for u in range(G):
        edges = nn(near_ref[u, :, :E], ends)
        for v in range(G):
            at = (v + SPAN) * B
            shifts[u, :, at : at + B] = jnp.where(v > place[0], edges[:, B:], edges[:, :B])
    put_band(place[1], place[0] + 2, 2 * G)
    for u in range(G):
        content = nt(near_ref[u, :, :E], keys)
        slope = nt(near_ref[u, :, E:], values)
        for v, apart in near_tiles(place, u):
            put_band(u, v, apart)
        pieces = []
        for v in range(G):
            at = (v + SPAN) * B
            both = content[:, v * B : (v + 1) * B] + shifts[u, :, at : at + B]
            pieces.append(jnp.where(lane < valid[G * v + place[1]], both, HIDDEN))
        scores = jnp.concatenate(pieces, axis=1)
        top = jnp.max(scores, axis=1, keepdims=True)
        weight = jnp.exp(scores - top)
        weight_ref[u * B : (u + 1) * B, :] = weight
        amount = jnp.sum(weight, axis=1, keepdims=True)
        mean = jnp.sum(weight * slope, axis=1, keepdims=True) / amount
        both = jnp.where(lane == 0, top + jnp.log(amount), jnp.where(lane == 1, mean, top))
        turned = both.T
        stats_ref[u : u + 1, :] = turned[0:1]
        stats_ref[G + u : G + u + 1, :] = turned[1:2]
        tops_ref[u : u + 1, :] = turned[2:3]


SCALARS = pl.BlockSpec(memory_space=pltpu.SMEM)
ARRAY = pl.BlockSpec(memory_space=pltpu.VMEM)


def statistics(place, valid, near, far, mine, theirs):
    return pl.pallas_call(
        stats_kernel,
        in_specs=[SCALARS] * 2 + [ARRAY] * 4,
        out_specs=[ARRAY] * 4,
        out_shape=(
            jax.ShapeDtypeStruct((N, N), F32),
            jax.ShapeDtypeStruct((2 * G, B), F32),
            jax.ShapeDtypeStruct((G, B), F32),
            jax.ShapeDtypeStruct((E, WIDE), BF),
        ),
        scratch_shapes=[pltpu.VMEM((G, B, N + 2 * SPAN * B), F32)],
        compiler_params=pltpu.CompilerParams(vmem_limit_bytes=LIMIT),
        name="statistics",
    )(place, valid, near, far, mine, theirs)


def grads_kernel(
    place,
    near_ref,
    far_ref,
    weight_ref,
    tops_ref,
    parts_ref,
    table_ref,
    far_out,
    near_out,
    keep_out,
    send_out,
    query_sum,
    table_sum,
    held,
):
    clip = place[2]
    parts = parts_ref[...]
    each = parts[:, :G]
    top = jnp.max(each, axis=0)
    total = top + jnp.log(jnp.sum(jnp.exp(each - top[None]), axis=0))
    mean = jnp.sum(jnp.exp(each - total[None]) * parts[:, G:], axis=0)
    rest = jnp.zeros((B - 2 * G, B), F32)
    columns = jnp.concatenate([jnp.exp(tops_ref[...] - total), mean, rest], axis=0).T
    table_sum[...] = jnp.zeros_like(table_sum)
    held[:, :, : SPAN * B] = jnp.zeros((G, B, SPAN * B), F32)
    held[:, :, SPAN * B + N :] = jnp.zeros((G, B, SPAN * B), F32)

    keys = far_ref[:, :B, :E].reshape(N, E)
    values = far_ref[:, :B, E:].reshape(N, E)
    low_end, high_end = table_ref[:, :B], table_ref[:, WIDE - B :]
    ends = jnp.concatenate([low_end, high_end, low_end, high_end], axis=1)
    row = lax.broadcasted_iota(jnp.int32, (B, B), 0)
    lane = lax.broadcasted_iota(jnp.int32, (B, B), 1)
    turn = (lane + row) % B
    early = lane + row < B
    lows, probs, turned = [], [], []
    end_sum = jnp.zeros((E, 4 * B), F32)

    def add_band(u, v, apart, flipped):
        spun = jnp.take_along_axis(held[u, :, block_at(v)], turn, axis=1)
        band = jnp.concatenate(
            [jnp.where(early, 0.0, spun), jnp.where(early, spun, 0.0)], axis=1
        ).astype(BF)
        table_sum[:, band_at(apart)] += nn(flipped[:E], band)
        return nt(band, table_ref[:, band_at(apart)])

    for u in range(G):
        paired = near_ref[u]
        flipped = paired.astype(F32).T.astype(BF)
        turned.append(flipped)
        factor = columns[:, u : u + 1]
        mean = columns[:, G + u : G + u + 1]
        slope = nt(paired[:, E:], values)
        prob = weight_ref[u * B : (u + 1) * B, :] * factor
        low = (prob * (slope - mean)).astype(BF)
        wide = low.astype(F32)
        held[u, :, SPAN * B : SPAN * B + N] = wide
        lower = jnp.zeros((B, B), F32)
        upper = jnp.zeros((B, B), F32)
        for v in range(G):
            apart = G * (v - place[0]) + place[1] - u
            piece = wide[:, v * B : (v + 1) * B]
            lower = lower + jnp.where(apart <= -REACH, piece, 0.0)
            upper = upper + jnp.where(apart >= REACH, piece, 0.0)
        outer = jnp.concatenate([lower, upper], axis=1)
        coarse = outer.astype(BF)
        fine = (outer - coarse.astype(F32)).astype(BF)
        outer = jnp.concatenate([coarse, fine], axis=1)
        end_sum = end_sum + nn(flipped[:E], outer)
        query_grad = nn(low, keys) + nt(outer, ends)
        for v, apart in near_tiles(place, u):
            query_grad = query_grad + add_band(u, v, apart, flipped)
        query_sum[u] = query_grad
        lows.append(low)
        probs.append(prob.astype(BF))
    flipped = near_ref[place[1]].astype(F32).T.astype(BF)
    query_sum[place[1]] += add_band(place[1], place[0] + 2, 2 * G, flipped)
    for u in range(G):
        query_low = (query_sum[u] * SCALE).astype(BF)
        near_out[u] = jnp.concatenate([query_low[:E], query_low[E:]], axis=1)
    both = jnp.concatenate(turned, axis=1)
    pairs = jnp.concatenate(
        [nn(both[:E], jnp.concatenate(lows, axis=0)), nn(both[E:], jnp.concatenate(probs, axis=0))],
        axis=0,
    )
    offsets = lax.broadcasted_iota(jnp.int32, (E, WIDE), 1) - (TABLE // 2 + PAD)
    terms = table_sum[...]
    tails = end_sum
    tails = tails[:, : 2 * B] + tails[:, 2 * B :]
    upper = jnp.sum(jnp.where(offsets >= clip, terms, 0.0), axis=1, keepdims=True)
    lower = jnp.sum(jnp.where(offsets <= -clip, terms, 0.0), axis=1, keepdims=True)
    upper = upper + jnp.sum(tails[:, B:], axis=1, keepdims=True)
    lower = lower + jnp.sum(tails[:, :B], axis=1, keepdims=True)
    table_sum[...] = jnp.where(offsets == clip, upper, jnp.where(offsets == -clip, lower, terms))
    first = place[1] % 2 == 0
    for slot in range(SLOTS):
        block = table_sum[:, pl.ds(slot_column(place, slot), B)]
        at = lane[:E] + (slot_column(place, slot) - (TABLE // 2 + PAD))
        block = jnp.where(jnp.abs(at) <= clip, block, 0.0)
        top, end = block[: E // 2], block[E // 2 :]
        left = jnp.concatenate([top[:, :E], end[:, :E]], axis=1)
        right = jnp.concatenate([top[:, E:], end[:, E:]], axis=1)
        keep_out[slot] = jnp.where(first, left, right)
        send_out[slot] = jnp.where(first, right, left).astype(BF)
    far_out[:, B:] = jnp.zeros((G, E // 2, B), BF)
    for y in range(G):
        far_out[y, :B] = pairs[:, y * B : (y + 1) * B].T.astype(BF)


def gradients(place, near, far, weight, tops, parts, table):
    return pl.pallas_call(
        grads_kernel,
        in_specs=[SCALARS] + [ARRAY] * 6,
        out_specs=[ARRAY] * 4,
        out_shape=(
            jax.ShapeDtypeStruct((G, ROWS, B), BF),
            jax.ShapeDtypeStruct((G, E, B), BF),
            jax.ShapeDtypeStruct((32, E // 2, B), F32),
            jax.ShapeDtypeStruct((32, E // 2, B), BF),
        ),
        scratch_shapes=[
            pltpu.VMEM((G, B, E), F32),
            pltpu.VMEM((E, WIDE), F32),
            pltpu.VMEM((G, B, N + 2 * SPAN * B), F32),
        ],
        compiler_params=pltpu.CompilerParams(vmem_limit_bytes=LIMIT),
        name="gradients",
    )(place, near, far, weight, tops, parts, table)


def unproject_kernel(far_ref, near_ref, weights_ref, out_ref, table_ref):
    total = jnp.sum(far_ref[...].astype(F32), axis=0)
    pairs = total[:B].astype(BF)
    table_ref[...] = total[B:]
    packed = jnp.sum(near_ref[...].astype(F32), axis=0).astype(BF)
    query = jnp.concatenate([packed[:, :E], packed[:, E:]], axis=0)
    terms = nn(query, weights_ref[:E]) + nn(pairs, weights_ref[E:])
    for h in range(G):
        out_ref[h] = terms[:, h * B : (h + 1) * B].astype(BF)


def unproject(far, near, weights):
    return pl.pallas_call(
        unproject_kernel,
        out_shape=(
            jax.ShapeDtypeStruct((G, B, B), BF),
            jax.ShapeDtypeStruct((E // 2, B), F32),
        ),
        compiler_params=pltpu.CompilerParams(vmem_limit_bytes=LIMIT),
        name="unproject",
    )(far, near, weights)


def exchange(parts, axis):
    return lax.all_to_all(parts, axis, 0, 0, tiled=True)


def to_all(shard):
    return jnp.broadcast_to(shard[None], (G,) + shard.shape)


def across(shard, stride):
    return lax.ppermute(shard, "near", [(i, i ^ stride) for i in range(G)])


def shards(frames, weights, offset_table, clip_range, valid_frames, context_grad):
    weight_rows = weights.reshape(3 * E, G * B)
    place = jnp.stack([lax.axis_index("far"), lax.axis_index("near"), clip_range[0]])
    turned = offset_table.T
    chunk = jnp.concatenate([turned[: E // 2], turned[E // 2 :]], axis=1)
    gathered = exchange(to_all(frames), "head")
    near, far = project(gathered, weight_rows, context_grad, chunk)
    far = exchange(far, "far")
    mine = far[:, B:]
    for stride in STRIDES:
        mine = jnp.concatenate([mine, across(mine, stride)], axis=0)
    theirs = across(mine, 1)
    near = exchange(near, "near")
    weight, stats, tops, table = statistics(place, valid_frames, near, far, mine, theirs)
    parts = exchange(to_all(stats), "near")
    far, near, keep, send = gradients(place, near, far, weight, tops, parts, table)
    total = keep + across(send, 1).astype(F32)
    for stride in reversed(STRIDES):
        half = total.shape[0] // 2
        arrived = across(total[half:].astype(BF), stride)
        total = total[:half] + arrived.astype(F32)
    far = far.at[:, B:].set(total.astype(BF))
    terms, table_part = unproject(exchange(far, "far"), exchange(near, "near"), weight_rows)
    table_grad = table_part.reshape(E // 2, 2, E).transpose(2, 1, 0).reshape(E, E)
    terms = exchange(terms, "head")
    input_grad = jnp.sum(terms.astype(F32), axis=0).astype(BF)
    return (input_grad, table_grad)


def solution(mesh):
    split = Mesh(mesh.devices.reshape(G, G, G), ("far", "near", "head"))
    seq = ("far", "near")
    placed = (
        P(seq, "head"),
        P(None, "head", None),
        P(seq, "head"),
        P("head"),
        P(),
        P(seq, "head"),
    )
    return jax.shard_map(
        shards,
        mesh=split,
        in_specs=placed,
        out_specs=(P(seq, "head"), P(seq, "head")),
        check_vma=False,
    )
```

```python
import jax
import jax.numpy as jnp
from jax import lax
from jax.experimental import pallas as pl
from jax.experimental.pallas import tpu as pltpu
from jax.sharding import Mesh
from jax.sharding import PartitionSpec as P

B = 128
G = 8
E = 64
N = B * G
TABLE = 4096
REACH = 17
PAD = 256
WIDE = TABLE + 2 * PAD
SCALE = E ** (-0.5)
SPAN = 2
HALF = B // 2
SHARE = HALF + B
CHUNK = E // 2
ROWS = B + E // 2
HIDDEN = -1e30
BF = jnp.bfloat16
F32 = jnp.float32
LIMIT = 32 * 1024 * 1024


def nt(a, b):
    return lax.dot_general(a, b, (((1,), (1,)), ((), ())), preferred_element_type=F32)


def nn(a, b):
    return lax.dot_general(a, b, (((1,), (0,)), ((), ())), preferred_element_type=F32)


def project_kernel(frames_ref, weights_ref, grad_ref, chunk_ref, near_ref, far_ref):
    total = jnp.zeros((B, 3 * E), F32)
    for h in range(G):
        total = total + nt(frames_ref[h], weights_ref[:, h * B : (h + 1) * B])
    low = total.astype(BF)
    scaled = (low[:, :E].astype(F32) * SCALE).astype(BF)
    paired = jnp.concatenate([scaled, grad_ref[...]], axis=1)
    for g in range(G):
        near_ref[g, :HALF] = paired[(g % 2) * HALF : (g % 2 + 1) * HALF]
        near_ref[g, HALF:] = jnp.zeros((B, B), BF)
        far_ref[g, :B] = low[:, E:]
        far_ref[g, B:] = chunk_ref[...]


def project(frames, weights, grad, chunk):
    return pl.pallas_call(
        project_kernel,
        out_shape=(
            jax.ShapeDtypeStruct((G, SHARE, B), BF),
            jax.ShapeDtypeStruct((G, ROWS, B), BF),
        ),
        compiler_params=pltpu.CompilerParams(vmem_limit_bytes=LIMIT),
        name="project",
    )(frames, weights, grad, chunk)


def near_tiles(place, u):
    shift = place[1] - u
    first = jnp.where(shift >= 0, -2, -1)
    return [(place[0] + first + w, G * (first + w) + shift) for w in range(4)]


def band_at(apart):
    return pl.ds(pl.multiple_of((apart + REACH) * B, B), 2 * B)


def block_at(v):
    return pl.ds(pl.multiple_of((v + SPAN) * B, B), B)


def stats_kernel(
    place,
    valid,
    mine_ref,
    theirs_ref,
    far_ref,
    weight_ref,
    near_ref,
    stats_ref,
    tops_ref,
    table_ref,
    shifts,
):
    clip = place[2]
    table_ref[:, :PAD] = jnp.zeros((E, PAD), BF)
    table_ref[:, WIDE - PAD :] = jnp.zeros((E, PAD), BF)
    first = place[1] % 2 == 0
    for g in range(G):
        mine = mine_ref[g, :HALF].astype(F32)
        theirs = theirs_ref[g, :HALF].astype(F32)
        near_ref[g, :HALF] = jnp.where(first, mine, theirs).astype(BF)
        near_ref[g, HALF:] = jnp.where(first, theirs, mine).astype(BF)
    for y in range(G):
        rows = slice(HALF + CHUNK * (y % 4), HALF + CHUNK * (y % 4 + 1))
        own = first if y < 4 else jnp.logical_not(first)
        for k in range(4):
            left, right = (
                jnp.where(own, mine_ref[g, rows].astype(F32), theirs_ref[g, rows].astype(F32))
                for g in (2 * k, 2 * k + 1)
            )
            top = jnp.concatenate([left[:, :E], right[:, :E]], axis=1)
            end = jnp.concatenate([left[:, E:], right[:, E:]], axis=1)
            at = PAD + (4 * y + k) * B
            table_ref[:, at : at + B] = jnp.concatenate([top, end], axis=0).astype(BF)
    offsets = lax.broadcasted_iota(jnp.int32, (E, WIDE), 1) - (TABLE // 2 + PAD)
    rows = table_ref[...].astype(F32)
    upper = jnp.sum(jnp.where(offsets == clip, rows, 0.0), axis=1, keepdims=True)
    lower = jnp.sum(jnp.where(offsets == -clip, rows, 0.0), axis=1, keepdims=True)
    rows = jnp.where(offsets >= clip, upper, jnp.where(offsets <= -clip, lower, rows))
    table_ref[...] = rows.astype(BF)

    keys = far_ref[:, :B, :E].reshape(N, E)
    values = far_ref[:, :B, E:].reshape(N, E)
    ends = jnp.concatenate([table_ref[:, :B], table_ref[:, WIDE - B :]], axis=1)
    lane = lax.broadcasted_iota(jnp.int32, (B, B), 1)
    row = lax.broadcasted_iota(jnp.int32, (B, B), 0)
    late = lane + row < B

    def put_band(u, v, apart):
        band = nn(near_ref[u, :, :E], table_ref[:, band_at(apart)])
        picked = jnp.where(late, band[:, B:], band[:, :B])
        shifts[u, :, block_at(v)] = pltpu.roll(picked, 0, 1, stride=1, stride_axis=0)

    for u in range(G):
        edges = nn(near_ref[u, :, :E], ends)
        for v in range(G):
            at = (v + SPAN) * B
            shifts[u, :, at : at + B] = jnp.where(v > place[0], edges[:, B:], edges[:, :B])
    put_band(place[1], place[0] + 2, 2 * G)
    for u in range(G):
        content = nt(near_ref[u, :, :E], keys)
        slope = nt(near_ref[u, :, E:], values)
        for v, apart in near_tiles(place, u):
            put_band(u, v, apart)
        pieces = []
        for v in range(G):
            at = (v + SPAN) * B
            both = content[:, v * B : (v + 1) * B] + shifts[u, :, at : at + B]
            pieces.append(jnp.where(lane < valid[G * v + place[1]], both, HIDDEN))
        scores = jnp.concatenate(pieces, axis=1)
        top = jnp.max(scores, axis=1, keepdims=True)
        weight = jnp.exp(scores - top)
        weight_ref[u * B : (u + 1) * B, :] = weight
        amount = jnp.sum(weight, axis=1, keepdims=True)
        mean = jnp.sum(weight * slope, axis=1, keepdims=True) / amount
        both = jnp.where(lane == 0, top + jnp.log(amount), jnp.where(lane == 1, mean, top))
        turned = both.T
        stats_ref[u : u + 1, :] = turned[0:1]
        stats_ref[G + u : G + u + 1, :] = turned[1:2]
        tops_ref[u : u + 1, :] = turned[2:3]


SCALARS = pl.BlockSpec(memory_space=pltpu.SMEM)
ARRAY = pl.BlockSpec(memory_space=pltpu.VMEM)


def statistics(place, valid, mine, theirs, far):
    return pl.pallas_call(
        stats_kernel,
        in_specs=[SCALARS] * 2 + [ARRAY] * 3,
        out_specs=[ARRAY] * 5,
        out_shape=(
            jax.ShapeDtypeStruct((N, N), F32),
            jax.ShapeDtypeStruct((G, B, B), BF),
            jax.ShapeDtypeStruct((2 * G, B), F32),
            jax.ShapeDtypeStruct((G, B), F32),
            jax.ShapeDtypeStruct((E, WIDE), BF),
        ),
        scratch_shapes=[pltpu.VMEM((G, B, N + 2 * SPAN * B), F32)],
        compiler_params=pltpu.CompilerParams(vmem_limit_bytes=LIMIT),
        name="statistics",
    )(place, valid, mine, theirs, far)


def grads_kernel(
    place,
    near_ref,
    far_ref,
    weight_ref,
    tops_ref,
    parts_ref,
    table_ref,
    far_out,
    near_out,
    keep_out,
    send_out,
    query_sum,
    table_sum,
    held,
):
    clip = place[2]
    parts = parts_ref[...]
    each = parts[:, :G]
    top = jnp.max(each, axis=0)
    total = top + jnp.log(jnp.sum(jnp.exp(each - top[None]), axis=0))
    mean = jnp.sum(jnp.exp(each - total[None]) * parts[:, G:], axis=0)
    rest = jnp.zeros((B - 2 * G, B), F32)
    columns = jnp.concatenate([jnp.exp(tops_ref[...] - total), mean, rest], axis=0).T
    table_sum[...] = jnp.zeros_like(table_sum)
    held[:, :, : SPAN * B] = jnp.zeros((G, B, SPAN * B), F32)
    held[:, :, SPAN * B + N :] = jnp.zeros((G, B, SPAN * B), F32)

    keys = far_ref[:, :B, :E].reshape(N, E)
    values = far_ref[:, :B, E:].reshape(N, E)
    low_end, high_end = table_ref[:, :B], table_ref[:, WIDE - B :]
    ends = jnp.concatenate([low_end, high_end, low_end, high_end], axis=1)
    row = lax.broadcasted_iota(jnp.int32, (B, B), 0)
    lane = lax.broadcasted_iota(jnp.int32, (B, B), 1)
    turn = (lane + row) % B
    early = lane + row < B
    lows, probs, turned = [], [], []
    end_sum = jnp.zeros((E, 4 * B), F32)

    def add_band(u, v, apart, flipped):
        spun = jnp.take_along_axis(held[u, :, block_at(v)], turn, axis=1)
        band = jnp.concatenate(
            [jnp.where(early, 0.0, spun), jnp.where(early, spun, 0.0)], axis=1
        ).astype(BF)
        table_sum[:, band_at(apart)] += nn(flipped[:E], band)
        return nt(band, table_ref[:, band_at(apart)])

    for u in range(G):
        paired = near_ref[u]
        flipped = paired.astype(F32).T.astype(BF)
        turned.append(flipped)
        factor = columns[:, u : u + 1]
        mean = columns[:, G + u : G + u + 1]
        slope = nt(paired[:, E:], values)
        prob = weight_ref[u * B : (u + 1) * B, :] * factor
        low = (prob * (slope - mean)).astype(BF)
        wide = low.astype(F32)
        held[u, :, SPAN * B : SPAN * B + N] = wide
        lower = jnp.zeros((B, B), F32)
        upper = jnp.zeros((B, B), F32)
        for v in range(G):
            apart = G * (v - place[0]) + place[1] - u
            piece = wide[:, v * B : (v + 1) * B]
            lower = lower + jnp.where(apart <= -REACH, piece, 0.0)
            upper = upper + jnp.where(apart >= REACH, piece, 0.0)
        outer = jnp.concatenate([lower, upper], axis=1)
        coarse = outer.astype(BF)
        fine = (outer - coarse.astype(F32)).astype(BF)
        outer = jnp.concatenate([coarse, fine], axis=1)
        end_sum = end_sum + nn(flipped[:E], outer)
        query_grad = nn(low, keys) + nt(outer, ends)
        for v, apart in near_tiles(place, u):
            query_grad = query_grad + add_band(u, v, apart, flipped)
        query_sum[u] = query_grad
        lows.append(low)
        probs.append(prob.astype(BF))
    flipped = near_ref[place[1]].astype(F32).T.astype(BF)
    query_sum[place[1]] += add_band(place[1], place[0] + 2, 2 * G, flipped)
    for u in range(G):
        query_low = (query_sum[u] * SCALE).astype(BF)
        near_out[u, :HALF] = jnp.concatenate([query_low[:E], query_low[E:]], axis=1)
    both = jnp.concatenate(turned, axis=1)
    pairs = jnp.concatenate(
        [nn(both[:E], jnp.concatenate(lows, axis=0)), nn(both[E:], jnp.concatenate(probs, axis=0))],
        axis=0,
    )
    offsets = lax.broadcasted_iota(jnp.int32, (E, WIDE), 1) - (TABLE // 2 + PAD)
    terms = table_sum[...]
    tails = end_sum
    tails = tails[:, : 2 * B] + tails[:, 2 * B :]
    upper = jnp.sum(jnp.where(offsets >= clip, terms, 0.0), axis=1, keepdims=True)
    lower = jnp.sum(jnp.where(offsets <= -clip, terms, 0.0), axis=1, keepdims=True)
    upper = upper + jnp.sum(tails[:, B:], axis=1, keepdims=True)
    lower = lower + jnp.sum(tails[:, :B], axis=1, keepdims=True)
    table_sum[...] = jnp.where(offsets == clip, upper, jnp.where(offsets == -clip, lower, terms))
    first = place[1] % 2 == 0
    for k in range(4):
        pieces = []
        for y in range(G):
            at = PAD + (4 * y + k) * B
            block = table_sum[:, at : at + B]
            block = jnp.where(jnp.abs(lane[:E] + (at - TABLE // 2 - PAD)) <= clip, block, 0.0)
            top, end = block[:CHUNK], block[CHUNK:]
            left = jnp.concatenate([top[:, :E], end[:, :E]], axis=1)
            right = jnp.concatenate([top[:, E:], end[:, E:]], axis=1)
            pieces.append((left, right))
        for y in range(4):
            rows = slice(CHUNK * y, CHUNK * (y + 1))
            for side in range(2):
                early_half, late_half = pieces[y][side], pieces[y + 4][side]
                keep_out[2 * k + side, rows] = jnp.where(first, early_half, late_half)
                send_out[2 * k + side, rows] = jnp.where(first, late_half, early_half).astype(BF)
    near_out[:, HALF:] = jnp.zeros((G, B, B), BF)
    for y in range(G):
        far_out[y] = pairs[:, y * B : (y + 1) * B].T.astype(BF)


def gradients(place, near, far, weight, tops, parts, table):
    return pl.pallas_call(
        grads_kernel,
        in_specs=[SCALARS] + [ARRAY] * 6,
        out_specs=[ARRAY] * 4,
        out_shape=(
            jax.ShapeDtypeStruct((G, B, B), BF),
            jax.ShapeDtypeStruct((G, SHARE, B), BF),
            jax.ShapeDtypeStruct((G, B, B), F32),
            jax.ShapeDtypeStruct((G, B, B), BF),
        ),
        scratch_shapes=[
            pltpu.VMEM((G, B, E), F32),
            pltpu.VMEM((E, WIDE), F32),
            pltpu.VMEM((G, B, N + 2 * SPAN * B), F32),
        ],
        compiler_params=pltpu.CompilerParams(vmem_limit_bytes=LIMIT),
        name="gradients",
    )(place, near, far, weight, tops, parts, table)


def fold_kernel(near_ref, pairs_ref, query_ref, far_ref):
    packed = jnp.sum(near_ref[:, :HALF].astype(F32), axis=0).astype(BF)
    query_ref[...] = jnp.concatenate([packed[:, :E], packed[:, E:]], axis=0)
    for side in range(2):
        total = near_ref[side, HALF:].astype(F32)
        for k in range(1, 4):
            total = total + near_ref[2 * k + side, HALF:].astype(F32)
        for y in range(4):
            far_ref[4 * side + y, B:] = total[CHUNK * y : CHUNK * (y + 1)].astype(BF)
    far_ref[:, :B] = pairs_ref[...]


def fold(near, pairs):
    return pl.pallas_call(
        fold_kernel,
        out_shape=(jax.ShapeDtypeStruct((B, E), BF), jax.ShapeDtypeStruct((G, ROWS, B), BF)),
        compiler_params=pltpu.CompilerParams(vmem_limit_bytes=LIMIT),
        name="fold",
    )(near, pairs)


def unproject_kernel(far_ref, query_ref, weights_ref, out_ref, table_ref):
    total = jnp.sum(far_ref[...].astype(F32), axis=0)
    pairs = total[:B].astype(BF)
    table_ref[...] = total[B:]
    terms = nn(query_ref[...], weights_ref[:E]) + nn(pairs, weights_ref[E:])
    for h in range(G):
        out_ref[h] = terms[:, h * B : (h + 1) * B].astype(BF)


def unproject(far, query, weights):
    return pl.pallas_call(
        unproject_kernel,
        out_shape=(
            jax.ShapeDtypeStruct((G, B, B), BF),
            jax.ShapeDtypeStruct((E // 2, B), F32),
        ),
        compiler_params=pltpu.CompilerParams(vmem_limit_bytes=LIMIT),
        name="unproject",
    )(far, query, weights)


def exchange(parts, axis):
    return lax.all_to_all(parts, axis, 0, 0, tiled=True)


def to_all(shard):
    return jnp.broadcast_to(shard[None], (G,) + shard.shape)


def other_core(shard):
    return lax.ppermute(shard, "near", [(i, i ^ 1) for i in range(G)])


def shards(frames, weights, offset_table, clip_range, valid_frames, context_grad):
    weight_rows = weights.reshape(3 * E, G * B)
    place = jnp.stack([lax.axis_index("far"), lax.axis_index("near"), clip_range[0]])
    turned = offset_table.T
    chunk = jnp.concatenate([turned[: E // 2], turned[E // 2 :]], axis=1)
    gathered = exchange(to_all(frames), "head")
    near, far = project(gathered, weight_rows, context_grad, chunk)
    far = exchange(far, "far")
    chunks = jnp.broadcast_to(far[:, B:].reshape(1, 2, B, B), (4, 2, B, B)).reshape(G, B, B)
    mine = exchange(near.at[:, HALF:].set(chunks), "near")
    theirs = other_core(mine)
    weight, near, stats, tops, table = statistics(place, valid_frames, mine, theirs, far)
    parts = exchange(to_all(stats), "near")
    pairs, near, keep, send = gradients(place, near, far, weight, tops, parts, table)
    halves = (keep + other_core(send).astype(F32)).astype(BF)
    query, far = fold(exchange(near.at[:, HALF:].set(halves), "near"), pairs)
    terms, table_part = unproject(exchange(far, "far"), query, weight_rows)
    table_grad = table_part.reshape(E // 2, 2, E).transpose(2, 1, 0).reshape(E, E)
    terms = exchange(terms, "head")
    input_grad = jnp.sum(terms.astype(F32), axis=0).astype(BF)
    return (input_grad, table_grad)


def solution(mesh):
    split = Mesh(mesh.devices.reshape(G, G, G), ("far", "near", "head"))
    seq = ("far", "near")
    placed = (
        P(seq, "head"),
        P(None, "head", None),
        P(seq, "head"),
        P("head"),
        P(),
        P(seq, "head"),
    )
    return jax.shard_map(
        shards,
        mesh=split,
        in_specs=placed,
        out_specs=(P(seq, "head"), P(seq, "head")),
        check_vma=False,
    )
```

```python
import jax
import jax.numpy as jnp
from jax import lax
from jax.experimental import pallas as pl
from jax.experimental.pallas import tpu as pltpu
from jax.sharding import Mesh
from jax.sharding import PartitionSpec as P

B = 128
G = 8
E = 64
N = B * G
TABLE = 4096
REACH = 17
PAD = 256
WIDE = TABLE + 2 * PAD
SCALE = E ** (-0.5)
SPAN = 2
HALF = B // 2
SHARE = HALF + B
CHUNK = E // 2
ROWS = B + E // 2
HIDDEN = -1e30
BF = jnp.bfloat16
F32 = jnp.float32
LIMIT = 32 * 1024 * 1024
SCALARS = pl.BlockSpec(memory_space=pltpu.SMEM)
ARRAY = pl.BlockSpec(memory_space=pltpu.VMEM)


def nt(a, b):
    return lax.dot_general(a, b, (((1,), (1,)), ((), ())), preferred_element_type=F32)


def nn(a, b):
    return lax.dot_general(a, b, (((1,), (0,)), ((), ())), preferred_element_type=F32)


def spread_kernel(frames_ref, out_ref, done):
    copies = [pltpu.make_async_copy(frames_ref, out_ref.at[g], done.at[g]) for g in range(G)]
    for copy in copies:
        copy.start()
    for copy in copies:
        copy.wait()


def spread(frames):
    return pl.pallas_call(
        spread_kernel,
        in_specs=[pl.BlockSpec(memory_space=pl.ANY)],
        out_specs=pl.BlockSpec(memory_space=pl.ANY),
        out_shape=jax.ShapeDtypeStruct((G,) + frames.shape, frames.dtype),
        scratch_shapes=[pltpu.SemaphoreType.DMA((G,))],
        name="spread",
    )(frames)


def prepare_kernel(place, valid, weights_ref, copy_ref, live_ref):
    copy_ref[...] = weights_ref[...]
    lane = lax.broadcasted_iota(jnp.int32, (1, B), 1)
    for v in range(G):
        live_ref[v : v + 1, :] = jnp.where(lane < valid[G * v + place[1]], 1.0, 0.0)


def prepare(place, valid, weights):
    return pl.pallas_call(
        prepare_kernel,
        in_specs=[SCALARS] * 2 + [ARRAY],
        out_specs=[ARRAY] * 2,
        out_shape=(
            jax.ShapeDtypeStruct(weights.shape, BF),
            jax.ShapeDtypeStruct((G, B), F32),
        ),
        cost_estimate=pl.CostEstimate(flops=0, bytes_accessed=1 << 21, transcendentals=0),
        name="prepare",
    )(place, valid, weights)


def project_kernel(frames_ref, weights_ref, grad_ref, chunk_ref, near_ref, far_ref):
    total = jnp.zeros((B, 3 * E), F32)
    for h in range(G):
        total = total + nt(frames_ref[h], weights_ref[:, h * B : (h + 1) * B])
    low = total.astype(BF)
    scaled = (low[:, :E].astype(F32) * SCALE).astype(BF)
    paired = jnp.concatenate([scaled, grad_ref[...]], axis=1)
    for g in range(G):
        near_ref[g, :HALF] = paired[(g % 2) * HALF : (g % 2 + 1) * HALF]
        near_ref[g, HALF:] = jnp.zeros((B, B), BF)
        far_ref[g, :B] = low[:, E:]
        far_ref[g, B:] = chunk_ref[...]


def project(frames, weights, grad, chunk):
    return pl.pallas_call(
        project_kernel,
        out_shape=(
            jax.ShapeDtypeStruct((G, SHARE, B), BF),
            jax.ShapeDtypeStruct((G, ROWS, B), BF),
        ),
        compiler_params=pltpu.CompilerParams(vmem_limit_bytes=LIMIT),
        name="project",
    )(frames, weights, grad, chunk)


def near_tiles(place, u):
    shift = place[1] - u
    first = jnp.where(shift >= 0, -2, -1)
    return [(place[0] + first + w, G * (first + w) + shift) for w in range(4)]


def band_at(apart):
    return pl.ds(pl.multiple_of((apart + REACH) * B, B), 2 * B)


def block_at(v):
    return pl.ds(pl.multiple_of((v + SPAN) * B, B), B)


def stats_kernel(
    place,
    live_ref,
    mine_ref,
    theirs_ref,
    far_ref,
    weight_ref,
    slope_ref,
    near_ref,
    stats_ref,
    tops_ref,
    table_ref,
    shifts,
    content_ref,
):
    clip = place[2]
    table_ref[:, :PAD] = jnp.zeros((E, PAD), BF)
    table_ref[:, WIDE - PAD :] = jnp.zeros((E, PAD), BF)
    first = place[1] % 2 == 0
    for g in range(G):
        mine = mine_ref[g, :HALF].astype(F32)
        theirs = theirs_ref[g, :HALF].astype(F32)
        near_ref[g, :HALF] = jnp.where(first, mine, theirs).astype(BF)
        near_ref[g, HALF:] = jnp.where(first, theirs, mine).astype(BF)
    for y in range(G):
        rows = slice(HALF + CHUNK * (y % 4), HALF + CHUNK * (y % 4 + 1))
        own = first if y < 4 else jnp.logical_not(first)
        for k in range(4):
            left, right = (
                jnp.where(own, mine_ref[g, rows].astype(F32), theirs_ref[g, rows].astype(F32))
                for g in (2 * k, 2 * k + 1)
            )
            top = jnp.concatenate([left[:, :E], right[:, :E]], axis=1)
            end = jnp.concatenate([left[:, E:], right[:, E:]], axis=1)
            at = PAD + (4 * y + k) * B
            table_ref[:, at : at + B] = jnp.concatenate([top, end], axis=0).astype(BF)
    offsets = lax.broadcasted_iota(jnp.int32, (E, WIDE), 1) - (TABLE // 2 + PAD)
    rows = table_ref[...].astype(F32)
    upper = jnp.sum(jnp.where(offsets == clip, rows, 0.0), axis=1, keepdims=True)
    lower = jnp.sum(jnp.where(offsets == -clip, rows, 0.0), axis=1, keepdims=True)
    rows = jnp.where(offsets >= clip, upper, jnp.where(offsets <= -clip, lower, rows))
    table_ref[...] = rows.astype(BF)

    keys = far_ref[:, :B, :E].reshape(N, E)
    values = far_ref[:, :B, E:].reshape(N, E)
    ends = jnp.concatenate([table_ref[:, :B], table_ref[:, WIDE - B :]], axis=1)
    lane = lax.broadcasted_iota(jnp.int32, (B, B), 1)
    row = lax.broadcasted_iota(jnp.int32, (B, B), 0)
    late = lane + row < B

    def put_band(u, v, apart):
        band = nn(near_ref[u, :, :E], table_ref[:, band_at(apart)])
        picked = jnp.where(late, band[:, B:], band[:, :B])
        shifts[u, :, block_at(v)] = pltpu.roll(picked, 0, 1, stride=1, stride_axis=0)

    for u in range(G):
        edges = nn(near_ref[u, :, :E], ends)
        for v in range(G):
            at = (v + SPAN) * B
            shifts[u, :, at : at + B] = jnp.where(v > place[0], edges[:, B:], edges[:, :B])
    put_band(place[1], place[0] + 2, 2 * G)
    queries = near_ref[:, :, :E].reshape(N, E)
    grads = near_ref[:, :, E:].reshape(N, E)
    for at in range(0, N, 2 * B):
        content_ref[:, at : at + 2 * B] = nt(queries, keys[at : at + 2 * B])
        slope_ref[:, at : at + 2 * B] = nt(grads, values[at : at + 2 * B])
    for u in range(G):
        rows = slice(u * B, (u + 1) * B)
        for v, apart in near_tiles(place, u):
            put_band(u, v, apart)
        pieces = []
        for v in range(G):
            at = (v + SPAN) * B
            both = content_ref[rows, v * B : (v + 1) * B] + shifts[u, :, at : at + B]
            pieces.append(jnp.where(live_ref[v : v + 1, :] > 0.0, both, HIDDEN))
        scores = jnp.concatenate(pieces, axis=1)
        top = jnp.max(scores, axis=1, keepdims=True)
        weight = jnp.exp(scores - top)
        weight_ref[rows, :] = weight
        amount = jnp.sum(weight, axis=1, keepdims=True)
        mean = jnp.sum(weight * slope_ref[rows, :], axis=1, keepdims=True) / amount
        both = jnp.where(lane == 0, top + jnp.log(amount), jnp.where(lane == 1, mean, top))
        turned = both.T
        stats_ref[u : u + 1, :] = turned[0:1]
        stats_ref[G + u : G + u + 1, :] = turned[1:2]
        tops_ref[u : u + 1, :] = turned[2:3]


def statistics(place, live, mine, theirs, far):
    return pl.pallas_call(
        stats_kernel,
        in_specs=[SCALARS] + [ARRAY] * 4,
        out_specs=[ARRAY] * 6,
        out_shape=(
            jax.ShapeDtypeStruct((N, N), F32),
            jax.ShapeDtypeStruct((N, N), F32),
            jax.ShapeDtypeStruct((G, B, B), BF),
            jax.ShapeDtypeStruct((2 * G, B), F32),
            jax.ShapeDtypeStruct((G, B), F32),
            jax.ShapeDtypeStruct((E, WIDE), BF),
        ),
        scratch_shapes=[pltpu.VMEM((G, B, N + 2 * SPAN * B), F32), pltpu.VMEM((N, N), F32)],
        compiler_params=pltpu.CompilerParams(vmem_limit_bytes=LIMIT),
        name="statistics",
    )(place, live, mine, theirs, far)


def grads_kernel(
    place,
    near_ref,
    far_ref,
    weight_ref,
    slope_ref,
    tops_ref,
    parts_ref,
    table_ref,
    far_out,
    near_out,
    keep_out,
    send_out,
    query_sum,
    table_sum,
    held,
    lows,
    probs,
    outers,
):
    clip = place[2]
    parts = parts_ref[...]
    each = parts[:, :G]
    top = jnp.max(each, axis=0)
    total = top + jnp.log(jnp.sum(jnp.exp(each - top[None]), axis=0))
    mean = jnp.sum(jnp.exp(each - total[None]) * parts[:, G:], axis=0)
    rest = jnp.zeros((B - 2 * G, B), F32)
    columns = jnp.concatenate([jnp.exp(tops_ref[...] - total), mean, rest], axis=0).T
    table_sum[...] = jnp.zeros_like(table_sum)
    held[:, :, : SPAN * B] = jnp.zeros((G, B, SPAN * B), F32)
    held[:, :, SPAN * B + N :] = jnp.zeros((G, B, SPAN * B), F32)

    keys = far_ref[:, :B, :E].reshape(N, E)
    low_end, high_end = table_ref[:, :B], table_ref[:, WIDE - B :]
    ends = jnp.concatenate([low_end, high_end, low_end, high_end], axis=1)
    row = lax.broadcasted_iota(jnp.int32, (B, B), 0)
    lane = lax.broadcasted_iota(jnp.int32, (B, B), 1)
    turn = (lane + row) % B
    early = lane + row < B
    turned = []

    def add_band(u, v, apart, flipped):
        spun = jnp.take_along_axis(held[u, :, block_at(v)], turn, axis=1)
        band = jnp.concatenate(
            [jnp.where(early, 0.0, spun), jnp.where(early, spun, 0.0)], axis=1
        ).astype(BF)
        table_sum[:, band_at(apart)] += nn(flipped[:E], band)
        return nt(band, table_ref[:, band_at(apart)])

    for u in range(G):
        paired = near_ref[u]
        flipped = paired.astype(F32).T.astype(BF)
        turned.append(flipped)
        factor = columns[:, u : u + 1]
        mean = columns[:, G + u : G + u + 1]
        rows = slice(u * B, (u + 1) * B)
        prob = weight_ref[rows, :] * factor
        low = (prob * (slope_ref[rows, :] - mean)).astype(BF)
        lows[rows, :] = low
        probs[rows, :] = prob.astype(BF)
        wide = low.astype(F32)
        held[u, :, SPAN * B : SPAN * B + N] = wide
        lower = jnp.zeros((B, B), F32)
        upper = jnp.zeros((B, B), F32)
        for v in range(G):
            apart = G * (v - place[0]) + place[1] - u
            piece = wide[:, v * B : (v + 1) * B]
            lower = lower + jnp.where(apart <= -REACH, piece, 0.0)
            upper = upper + jnp.where(apart >= REACH, piece, 0.0)
        outer = jnp.concatenate([lower, upper], axis=1)
        coarse = outer.astype(BF)
        fine = (outer - coarse.astype(F32)).astype(BF)
        outers[rows, :] = jnp.concatenate([coarse, fine], axis=1)
        query_sum[u] = sum(add_band(u, v, apart, flipped) for v, apart in near_tiles(place, u))
    flipped = near_ref[place[1]].astype(F32).T.astype(BF)
    query_sum[place[1]] += add_band(place[1], place[0] + 2, 2 * G, flipped)
    both = jnp.concatenate(turned, axis=1)
    main = nn(lows[...], keys) + nt(outers[...], ends)
    tails = nn(both[:E], outers[...])
    for u in range(G):
        query_low = ((query_sum[u] + main[u * B : (u + 1) * B]) * SCALE).astype(BF)
        near_out[u, :HALF] = jnp.concatenate([query_low[:E], query_low[E:]], axis=1)
    pairs = jnp.concatenate([nn(both[:E], lows[...]), nn(both[E:], probs[...])], axis=0)
    offsets = lax.broadcasted_iota(jnp.int32, (E, WIDE), 1) - (TABLE // 2 + PAD)
    terms = table_sum[...]
    tails = tails[:, : 2 * B] + tails[:, 2 * B :]
    upper = jnp.sum(jnp.where(offsets >= clip, terms, 0.0), axis=1, keepdims=True)
    lower = jnp.sum(jnp.where(offsets <= -clip, terms, 0.0), axis=1, keepdims=True)
    upper = upper + jnp.sum(tails[:, B:], axis=1, keepdims=True)
    lower = lower + jnp.sum(tails[:, :B], axis=1, keepdims=True)
    table_sum[...] = jnp.where(offsets == clip, upper, jnp.where(offsets == -clip, lower, terms))
    first = place[1] % 2 == 0
    for k in range(4):
        pieces = []
        for y in range(G):
            at = PAD + (4 * y + k) * B
            block = table_sum[:, at : at + B]
            block = jnp.where(jnp.abs(lane[:E] + (at - TABLE // 2 - PAD)) <= clip, block, 0.0)
            top, end = block[:CHUNK], block[CHUNK:]
            left = jnp.concatenate([top[:, :E], end[:, :E]], axis=1)
            right = jnp.concatenate([top[:, E:], end[:, E:]], axis=1)
            pieces.append((left, right))
        for y in range(4):
            rows = slice(CHUNK * y, CHUNK * (y + 1))
            for side in range(2):
                early_half, late_half = pieces[y][side], pieces[y + 4][side]
                keep_out[2 * k + side, rows] = jnp.where(first, early_half, late_half)
                send_out[2 * k + side, rows] = jnp.where(first, late_half, early_half).astype(BF)
    near_out[:, HALF:] = jnp.zeros((G, B, B), BF)
    for y in range(G):
        far_out[y] = pairs[:, y * B : (y + 1) * B].T.astype(BF)


def gradients(place, near, far, weight, slope, tops, parts, table):
    return pl.pallas_call(
        grads_kernel,
        in_specs=[SCALARS] + [ARRAY] * 7,
        out_specs=[ARRAY] * 4,
        out_shape=(
            jax.ShapeDtypeStruct((G, B, B), BF),
            jax.ShapeDtypeStruct((G, SHARE, B), BF),
            jax.ShapeDtypeStruct((G, B, B), F32),
            jax.ShapeDtypeStruct((G, B, B), BF),
        ),
        scratch_shapes=[
            pltpu.VMEM((G, B, E), F32),
            pltpu.VMEM((E, WIDE), F32),
            pltpu.VMEM((G, B, N + 2 * SPAN * B), F32),
            pltpu.VMEM((N, N), BF),
            pltpu.VMEM((N, N), BF),
            pltpu.VMEM((N, 4 * B), BF),
        ],
        compiler_params=pltpu.CompilerParams(vmem_limit_bytes=LIMIT),
        name="gradients",
    )(place, near, far, weight, slope, tops, parts, table)


def fold_kernel(near_ref, pairs_ref, query_ref, far_ref):
    packed = jnp.sum(near_ref[:, :HALF].astype(F32), axis=0).astype(BF)
    query_ref[...] = jnp.concatenate([packed[:, :E], packed[:, E:]], axis=0)
    for side in range(2):
        total = near_ref[side, HALF:].astype(F32)
        for k in range(1, 4):
            total = total + near_ref[2 * k + side, HALF:].astype(F32)
        for y in range(4):
            far_ref[4 * side + y, B:] = total[CHUNK * y : CHUNK * (y + 1)].astype(BF)
    far_ref[:, :B] = pairs_ref[...]


def fold(near, pairs):
    return pl.pallas_call(
        fold_kernel,
        out_shape=(jax.ShapeDtypeStruct((B, E), BF), jax.ShapeDtypeStruct((G, ROWS, B), BF)),
        compiler_params=pltpu.CompilerParams(vmem_limit_bytes=LIMIT),
        name="fold",
    )(near, pairs)


def unproject_kernel(far_ref, query_ref, weights_ref, out_ref, table_ref):
    total = jnp.sum(far_ref[...].astype(F32), axis=0)
    pairs = total[:B].astype(BF)
    table_ref[...] = total[B:]
    terms = nn(query_ref[...], weights_ref[:E]) + nn(pairs, weights_ref[E:])
    for h in range(G):
        out_ref[h] = terms[:, h * B : (h + 1) * B].astype(BF)


def unproject(far, query, weights):
    return pl.pallas_call(
        unproject_kernel,
        out_shape=(
            jax.ShapeDtypeStruct((G, B, B), BF),
            jax.ShapeDtypeStruct((E // 2, B), F32),
        ),
        compiler_params=pltpu.CompilerParams(vmem_limit_bytes=LIMIT),
        name="unproject",
    )(far, query, weights)


def exchange(parts, axis):
    return lax.all_to_all(parts, axis, 0, 0, tiled=True)


def to_all(shard):
    return jnp.broadcast_to(shard[None], (G,) + shard.shape)


def other_core(shard):
    return lax.ppermute(shard, "near", [(i, i ^ 1) for i in range(G)])


def shards(frames, weights, offset_table, clip_range, valid_frames, context_grad):
    weight_rows = weights.reshape(3 * E, G * B)
    place = jnp.stack([lax.axis_index("far"), lax.axis_index("near"), clip_range[0]])
    turned = offset_table.T
    chunk = jnp.concatenate([turned[: E // 2], turned[E // 2 :]], axis=1)
    early_weights, live = prepare(place, valid_frames, weight_rows)
    gathered = exchange(spread(frames), "head")
    near, far = project(gathered, early_weights, context_grad, chunk)
    far = exchange(far, "far")
    chunks = jnp.broadcast_to(far[:, B:].reshape(1, 2, B, B), (4, 2, B, B)).reshape(G, B, B)
    mine = exchange(near.at[:, HALF:].set(chunks), "near")
    theirs = other_core(mine)
    weight, slope, near, stats, tops, table = statistics(place, live, mine, theirs, far)
    parts = exchange(to_all(stats), "near")
    pairs, near, keep, send = gradients(
        place, near, far, weight, slope, tops, parts, table
    )
    halves = (keep + other_core(send).astype(F32)).astype(BF)
    query, far = fold(exchange(near.at[:, HALF:].set(halves), "near"), pairs)
    terms, table_part = unproject(exchange(far, "far"), query, weight_rows)
    table_grad = table_part.reshape(E // 2, 2, E).transpose(2, 1, 0).reshape(E, E)
    terms = exchange(terms, "head")
    input_grad = jnp.sum(terms.astype(F32), axis=0).astype(BF)
    return (input_grad, table_grad)


def solution(mesh):
    split = Mesh(mesh.devices.reshape(G, G, G), ("far", "near", "head"))
    seq = ("far", "near")
    placed = (
        P(seq, "head"),
        P(None, "head", None),
        P(seq, "head"),
        P("head"),
        P(),
        P(seq, "head"),
    )
    return jax.shard_map(
        shards,
        mesh=split,
        in_specs=placed,
        out_specs=(P(seq, "head"), P(seq, "head")),
        check_vma=False,
    )
```

```python
import jax
import jax.numpy as jnp
from jax import lax
from jax.experimental import pallas as pl
from jax.experimental.pallas import tpu as pltpu
from jax.sharding import Mesh
from jax.sharding import PartitionSpec as P

B = 128
G = 8
E = 64
N = B * G
TABLE = 4096
REACH = 17
PAD = 256
WIDE = TABLE + 2 * PAD
SCALE = E ** (-0.5)
SPAN = 2
HALF = B // 2
SHARE = HALF + B
CHUNK = E // 2
ROWS = B + E // 2
HIDDEN = -1e30
BF = jnp.bfloat16
F32 = jnp.float32
LIMIT = 32 * 1024 * 1024
SCALARS = pl.BlockSpec(memory_space=pltpu.SMEM)
ARRAY = pl.BlockSpec(memory_space=pltpu.VMEM)


def nt(a, b):
    return lax.dot_general(a, b, (((1,), (1,)), ((), ())), preferred_element_type=F32)


def nn(a, b):
    return lax.dot_general(a, b, (((1,), (0,)), ((), ())), preferred_element_type=F32)


def project_kernel(frames_ref, weights_ref, grad_ref, chunk_ref, near_ref, far_ref):
    total = jnp.zeros((B, 3 * E), F32)
    for h in range(G):
        total = total + nt(frames_ref[h], weights_ref[:, h * B : (h + 1) * B])
    low = total.astype(BF)
    scaled = (low[:, :E].astype(F32) * SCALE).astype(BF)
    paired = jnp.concatenate([scaled, grad_ref[...]], axis=1)
    for g in range(G):
        near_ref[g, :HALF] = paired[(g % 2) * HALF : (g % 2 + 1) * HALF]
        near_ref[g, HALF:] = jnp.zeros((B, B), BF)
        far_ref[g, :B] = low[:, E:]
        far_ref[g, B:] = chunk_ref[...]


def project(frames, weights, grad, chunk):
    return pl.pallas_call(
        project_kernel,
        out_shape=(
            jax.ShapeDtypeStruct((G, SHARE, B), BF),
            jax.ShapeDtypeStruct((G, ROWS, B), BF),
        ),
        compiler_params=pltpu.CompilerParams(vmem_limit_bytes=LIMIT),
        name="project",
    )(frames, weights, grad, chunk)


def near_tiles(place, u):
    shift = place[1] - u
    first = jnp.where(shift >= 0, -2, -1)
    return [(place[0] + first + w, G * (first + w) + shift) for w in range(4)]


def band_at(apart):
    return pl.ds(pl.multiple_of((apart + REACH) * B, B), 2 * B)


def block_at(v):
    return pl.ds(pl.multiple_of((v + SPAN) * B, B), B)


def stats_kernel(
    place,
    mine_ref,
    theirs_ref,
    far_ref,
    weight_ref,
    slope_ref,
    near_ref,
    stats_ref,
    tops_ref,
    table_ref,
    shifts,
    content_ref,
):
    clip = place[2]
    table_ref[:, :PAD] = jnp.zeros((E, PAD), BF)
    table_ref[:, WIDE - PAD :] = jnp.zeros((E, PAD), BF)
    first = place[1] % 2 == 0
    for g in range(G):
        mine = mine_ref[g, :HALF].astype(F32)
        theirs = theirs_ref[g, :HALF].astype(F32)
        near_ref[g, :HALF] = jnp.where(first, mine, theirs).astype(BF)
        near_ref[g, HALF:] = jnp.where(first, theirs, mine).astype(BF)
    for y in range(G):
        rows = slice(HALF + CHUNK * (y % 4), HALF + CHUNK * (y % 4 + 1))
        own = first if y < 4 else jnp.logical_not(first)
        for k in range(4):
            left, right = (
                jnp.where(own, mine_ref[g, rows].astype(F32), theirs_ref[g, rows].astype(F32))
                for g in (2 * k, 2 * k + 1)
            )
            top = jnp.concatenate([left[:, :E], right[:, :E]], axis=1)
            end = jnp.concatenate([left[:, E:], right[:, E:]], axis=1)
            at = PAD + (4 * y + k) * B
            table_ref[:, at : at + B] = jnp.concatenate([top, end], axis=0).astype(BF)
    offsets = lax.broadcasted_iota(jnp.int32, (E, WIDE), 1) - (TABLE // 2 + PAD)
    rows = table_ref[...].astype(F32)
    upper = jnp.sum(jnp.where(offsets == clip, rows, 0.0), axis=1, keepdims=True)
    lower = jnp.sum(jnp.where(offsets == -clip, rows, 0.0), axis=1, keepdims=True)
    rows = jnp.where(offsets >= clip, upper, jnp.where(offsets <= -clip, lower, rows))
    table_ref[...] = rows.astype(BF)

    keys = far_ref[:, :B, :E].reshape(N, E)
    values = far_ref[:, :B, E:].reshape(N, E)
    ends = jnp.concatenate([table_ref[:, :B], table_ref[:, WIDE - B :]], axis=1)
    lane = lax.broadcasted_iota(jnp.int32, (B, B), 1)
    row = lax.broadcasted_iota(jnp.int32, (B, B), 0)
    late = lane + row < B

    def put_band(u, v, apart):
        band = nn(near_ref[u, :, :E], table_ref[:, band_at(apart)])
        picked = jnp.where(late, band[:, B:], band[:, :B])
        shifts[u, :, block_at(v)] = pltpu.roll(picked, 0, 1, stride=1, stride_axis=0)

    for u in range(G):
        edges = nn(near_ref[u, :, :E], ends)
        for v in range(G):
            at = (v + SPAN) * B
            shifts[u, :, at : at + B] = jnp.where(v > place[0], edges[:, B:], edges[:, :B])
    put_band(place[1], place[0] + 2, 2 * G)
    queries = near_ref[:, :, :E].reshape(N, E)
    grads = near_ref[:, :, E:].reshape(N, E)
    for at in range(0, N, 2 * B):
        content_ref[:, at : at + 2 * B] = nt(queries, keys[at : at + 2 * B])
        slope_ref[:, at : at + 2 * B] = nt(grads, values[at : at + 2 * B])
    for u in range(G):
        rows = slice(u * B, (u + 1) * B)
        for v, apart in near_tiles(place, u):
            put_band(u, v, apart)
        pieces = []
        for v in range(G):
            at = (v + SPAN) * B
            both = content_ref[rows, v * B : (v + 1) * B] + shifts[u, :, at : at + B]
            pieces.append(jnp.where(lane < place[3 + G * v + place[1]], both, HIDDEN))
        scores = jnp.concatenate(pieces, axis=1)
        top = jnp.max(scores, axis=1, keepdims=True)
        weight = jnp.exp(scores - top)
        weight_ref[rows, :] = weight
        amount = jnp.sum(weight, axis=1, keepdims=True)
        mean = jnp.sum(weight * slope_ref[rows, :], axis=1, keepdims=True) / amount
        both = jnp.where(lane == 0, top + jnp.log(amount), jnp.where(lane == 1, mean, top))
        turned = both.T
        stats_ref[u : u + 1, :] = turned[0:1]
        stats_ref[G + u : G + u + 1, :] = turned[1:2]
        tops_ref[u : u + 1, :] = turned[2:3]


def statistics(place, mine, theirs, far):
    return pl.pallas_call(
        stats_kernel,
        in_specs=[SCALARS] + [ARRAY] * 3,
        out_specs=[ARRAY] * 6,
        out_shape=(
            jax.ShapeDtypeStruct((N, N), F32),
            jax.ShapeDtypeStruct((N, N), F32),
            jax.ShapeDtypeStruct((G, B, B), BF),
            jax.ShapeDtypeStruct((2 * G, B), F32),
            jax.ShapeDtypeStruct((G, B), F32),
            jax.ShapeDtypeStruct((E, WIDE), BF),
        ),
        scratch_shapes=[pltpu.VMEM((G, B, N + 2 * SPAN * B), F32), pltpu.VMEM((N, N), F32)],
        compiler_params=pltpu.CompilerParams(vmem_limit_bytes=LIMIT),
        name="statistics",
    )(place, mine, theirs, far)


def grads_kernel(
    place,
    near_ref,
    far_ref,
    weight_ref,
    slope_ref,
    tops_ref,
    parts_ref,
    table_ref,
    far_out,
    near_out,
    keep_out,
    send_out,
    query_sum,
    table_sum,
    held,
    lows,
    probs,
    outers,
):
    clip = place[2]
    parts = parts_ref[...]
    each = parts[:, :G]
    top = jnp.max(each, axis=0)
    total = top + jnp.log(jnp.sum(jnp.exp(each - top[None]), axis=0))
    mean = jnp.sum(jnp.exp(each - total[None]) * parts[:, G:], axis=0)
    rest = jnp.zeros((B - 2 * G, B), F32)
    columns = jnp.concatenate([jnp.exp(tops_ref[...] - total), mean, rest], axis=0).T
    table_sum[...] = jnp.zeros_like(table_sum)
    held[:, :, : SPAN * B] = jnp.zeros((G, B, SPAN * B), F32)
    held[:, :, SPAN * B + N :] = jnp.zeros((G, B, SPAN * B), F32)

    keys = far_ref[:, :B, :E].reshape(N, E)
    low_end, high_end = table_ref[:, :B], table_ref[:, WIDE - B :]
    ends = jnp.concatenate([low_end, high_end, low_end, high_end], axis=1)
    row = lax.broadcasted_iota(jnp.int32, (B, B), 0)
    lane = lax.broadcasted_iota(jnp.int32, (B, B), 1)
    turn = (lane + row) % B
    early = lane + row < B
    turned = []

    def add_band(u, v, apart, flipped):
        spun = jnp.take_along_axis(held[u, :, block_at(v)], turn, axis=1)
        band = jnp.concatenate(
            [jnp.where(early, 0.0, spun), jnp.where(early, spun, 0.0)], axis=1
        ).astype(BF)
        table_sum[:, band_at(apart)] += nn(flipped[:E], band)
        return nt(band, table_ref[:, band_at(apart)])

    for u in range(G):
        paired = near_ref[u]
        flipped = paired.astype(F32).T.astype(BF)
        turned.append(flipped)
        factor = columns[:, u : u + 1]
        mean = columns[:, G + u : G + u + 1]
        rows = slice(u * B, (u + 1) * B)
        prob = weight_ref[rows, :] * factor
        low = (prob * (slope_ref[rows, :] - mean)).astype(BF)
        lows[rows, :] = low
        probs[rows, :] = prob.astype(BF)
        wide = low.astype(F32)
        held[u, :, SPAN * B : SPAN * B + N] = wide
        lower = jnp.zeros((B, B), F32)
        upper = jnp.zeros((B, B), F32)
        for v in range(G):
            apart = G * (v - place[0]) + place[1] - u
            piece = wide[:, v * B : (v + 1) * B]
            lower = lower + jnp.where(apart <= -REACH, piece, 0.0)
            upper = upper + jnp.where(apart >= REACH, piece, 0.0)
        outer = jnp.concatenate([lower, upper], axis=1)
        coarse = outer.astype(BF)
        fine = (outer - coarse.astype(F32)).astype(BF)
        outers[rows, :] = jnp.concatenate([coarse, fine], axis=1)
        query_sum[u] = sum(add_band(u, v, apart, flipped) for v, apart in near_tiles(place, u))
    flipped = near_ref[place[1]].astype(F32).T.astype(BF)
    query_sum[place[1]] += add_band(place[1], place[0] + 2, 2 * G, flipped)
    both = jnp.concatenate(turned, axis=1)
    main = nn(lows[...], keys) + nt(outers[...], ends)
    tails = nn(both[:E], outers[...])
    for u in range(G):
        query_low = ((query_sum[u] + main[u * B : (u + 1) * B]) * SCALE).astype(BF)
        near_out[u, :HALF] = jnp.concatenate([query_low[:E], query_low[E:]], axis=1)
    pairs = jnp.concatenate([nn(both[:E], lows[...]), nn(both[E:], probs[...])], axis=0)
    offsets = lax.broadcasted_iota(jnp.int32, (E, WIDE), 1) - (TABLE // 2 + PAD)
    terms = table_sum[...]
    tails = tails[:, : 2 * B] + tails[:, 2 * B :]
    upper = jnp.sum(jnp.where(offsets >= clip, terms, 0.0), axis=1, keepdims=True)
    lower = jnp.sum(jnp.where(offsets <= -clip, terms, 0.0), axis=1, keepdims=True)
    upper = upper + jnp.sum(tails[:, B:], axis=1, keepdims=True)
    lower = lower + jnp.sum(tails[:, :B], axis=1, keepdims=True)
    table_sum[...] = jnp.where(offsets == clip, upper, jnp.where(offsets == -clip, lower, terms))
    first = place[1] % 2 == 0
    for k in range(4):
        pieces = []
        for y in range(G):
            at = PAD + (4 * y + k) * B
            block = table_sum[:, at : at + B]
            block = jnp.where(jnp.abs(lane[:E] + (at - TABLE // 2 - PAD)) <= clip, block, 0.0)
            top, end = block[:CHUNK], block[CHUNK:]
            left = jnp.concatenate([top[:, :E], end[:, :E]], axis=1)
            right = jnp.concatenate([top[:, E:], end[:, E:]], axis=1)
            pieces.append((left, right))
        for y in range(4):
            rows = slice(CHUNK * y, CHUNK * (y + 1))
            for side in range(2):
                early_half, late_half = pieces[y][side], pieces[y + 4][side]
                keep_out[2 * k + side, rows] = jnp.where(first, early_half, late_half)
                send_out[2 * k + side, rows] = jnp.where(first, late_half, early_half).astype(BF)
    near_out[:, HALF:] = jnp.zeros((G, B, B), BF)
    for y in range(G):
        far_out[y] = pairs[:, y * B : (y + 1) * B].T.astype(BF)


def gradients(place, near, far, weight, slope, tops, parts, table):
    return pl.pallas_call(
        grads_kernel,
        in_specs=[SCALARS] + [ARRAY] * 7,
        out_specs=[ARRAY] * 4,
        out_shape=(
            jax.ShapeDtypeStruct((G, B, B), BF),
            jax.ShapeDtypeStruct((G, SHARE, B), BF),
            jax.ShapeDtypeStruct((G, B, B), F32),
            jax.ShapeDtypeStruct((G, B, B), BF),
        ),
        scratch_shapes=[
            pltpu.VMEM((G, B, E), F32),
            pltpu.VMEM((E, WIDE), F32),
            pltpu.VMEM((G, B, N + 2 * SPAN * B), F32),
            pltpu.VMEM((N, N), BF),
            pltpu.VMEM((N, N), BF),
            pltpu.VMEM((N, 4 * B), BF),
        ],
        compiler_params=pltpu.CompilerParams(vmem_limit_bytes=LIMIT),
        name="gradients",
    )(place, near, far, weight, slope, tops, parts, table)


def fold_kernel(near_ref, pairs_ref, query_ref, far_ref):
    packed = jnp.sum(near_ref[:, :HALF].astype(F32), axis=0).astype(BF)
    query_ref[...] = jnp.concatenate([packed[:, :E], packed[:, E:]], axis=0)
    for side in range(2):
        total = near_ref[side, HALF:].astype(F32)
        for k in range(1, 4):
            total = total + near_ref[2 * k + side, HALF:].astype(F32)
        for y in range(4):
            far_ref[4 * side + y, B:] = total[CHUNK * y : CHUNK * (y + 1)].astype(BF)
    far_ref[:, :B] = pairs_ref[...]


def fold(near, pairs):
    return pl.pallas_call(
        fold_kernel,
        out_shape=(jax.ShapeDtypeStruct((B, E), BF), jax.ShapeDtypeStruct((G, ROWS, B), BF)),
        compiler_params=pltpu.CompilerParams(vmem_limit_bytes=LIMIT),
        name="fold",
    )(near, pairs)


def unproject_kernel(far_ref, query_ref, weights_ref, out_ref, table_ref):
    total = jnp.sum(far_ref[...].astype(F32), axis=0)
    pairs = total[:B].astype(BF)
    table_ref[...] = total[B:]
    terms = nn(query_ref[...], weights_ref[:E]) + nn(pairs, weights_ref[E:])
    for h in range(G):
        out_ref[h] = terms[:, h * B : (h + 1) * B].astype(BF)


def unproject(far, query, weights):
    return pl.pallas_call(
        unproject_kernel,
        out_shape=(
            jax.ShapeDtypeStruct((G, B, B), BF),
            jax.ShapeDtypeStruct((E // 2, B), F32),
        ),
        compiler_params=pltpu.CompilerParams(vmem_limit_bytes=LIMIT),
        name="unproject",
    )(far, query, weights)


def exchange(parts, axis):
    return lax.all_to_all(parts, axis, 0, 0, tiled=True)


def to_all(shard):
    return jnp.broadcast_to(shard[None], (G,) + shard.shape)


def other_core(shard):
    return lax.ppermute(shard, "near", [(i, i ^ 1) for i in range(G)])


def shards(frames, weights, offset_table, clip_range, valid_frames, context_grad):
    weight_rows = weights.reshape(3 * E, G * B)
    own = jnp.stack([lax.axis_index("far"), lax.axis_index("near"), clip_range[0]])
    place = jnp.concatenate([own, valid_frames])
    turned = offset_table.T
    chunk = jnp.concatenate([turned[: E // 2], turned[E // 2 :]], axis=1)
    gathered = exchange(to_all(frames), "head")
    near, far = project(gathered, weight_rows, context_grad, chunk)
    far = exchange(far, "far")
    chunks = jnp.broadcast_to(far[:, B:].reshape(1, 2, B, B), (4, 2, B, B)).reshape(G, B, B)
    mine = exchange(near.at[:, HALF:].set(chunks), "near")
    theirs = other_core(mine)
    weight, slope, near, stats, tops, table = statistics(place, mine, theirs, far)
    parts = exchange(to_all(stats), "near")
    pairs, near, keep, send = gradients(
        place, near, far, weight, slope, tops, parts, table
    )
    halves = (keep + other_core(send).astype(F32)).astype(BF)
    query, far = fold(exchange(near.at[:, HALF:].set(halves), "near"), pairs)
    terms, table_part = unproject(exchange(far, "far"), query, weight_rows)
    table_grad = table_part.reshape(E // 2, 2, E).transpose(2, 1, 0).reshape(E, E)
    terms = exchange(terms, "head")
    input_grad = jnp.sum(terms.astype(F32), axis=0).astype(BF)
    return (input_grad, table_grad)


def solution(mesh):
    split = Mesh(mesh.devices.reshape(G, G, G), ("far", "near", "head"))
    seq = ("far", "near")
    placed = (
        P(seq, "head"),
        P(None, "head", None),
        P(seq, "head"),
        P("head"),
        P(),
        P(seq, "head"),
    )
    return jax.shard_map(
        shards,
        mesh=split,
        in_specs=placed,
        out_specs=(P(seq, "head"), P(seq, "head")),
        check_vma=False,
    )
```

```python
import jax
import jax.numpy as jnp
from jax import lax
from jax.experimental import pallas as pl
from jax.experimental.pallas import tpu as pltpu
from jax.sharding import Mesh
from jax.sharding import PartitionSpec as P

B = 128
G = 8
E = 64
N = B * G
TABLE = 4096
REACH = 17
PAD = 256
WIDE = TABLE + 2 * PAD
SCALE = E ** (-0.5)
SPAN = 2
PAIRS = 4
SHARE = B + 4 * E
BACK = E + 4 * E
CHUNK = E // 2
ROWS = B + E // 2
HIDDEN = -1e30
BF = jnp.bfloat16
F32 = jnp.float32
LIMIT = 32 * 1024 * 1024
SCALARS = pl.BlockSpec(memory_space=pltpu.SMEM)
ARRAY = pl.BlockSpec(memory_space=pltpu.VMEM)


def nt(a, b):
    return lax.dot_general(a, b, (((1,), (1,)), ((), ())), preferred_element_type=F32)


def nn(a, b):
    return lax.dot_general(a, b, (((1,), (0,)), ((), ())), preferred_element_type=F32)


def project_kernel(frames_ref, weights_ref, grad_ref, chunk_ref, near_ref, far_ref):
    total = jnp.zeros((B, 3 * E), F32)
    for h in range(G):
        total = total + nt(frames_ref[h], weights_ref[:, h * B : (h + 1) * B])
    low = total.astype(BF)
    scaled = (low[:, :E].astype(F32) * SCALE).astype(BF)
    paired = jnp.concatenate([scaled, grad_ref[...]], axis=1)
    for g in range(PAIRS):
        near_ref[g, :B] = paired
        near_ref[g, B:] = jnp.zeros((4 * E, B), BF)
    for g in range(G):
        far_ref[g, :B] = low[:, E:]
        far_ref[g, B:] = chunk_ref[...]


def project(frames, weights, grad, chunk):
    return pl.pallas_call(
        project_kernel,
        out_shape=(
            jax.ShapeDtypeStruct((PAIRS, SHARE, B), BF),
            jax.ShapeDtypeStruct((G, ROWS, B), BF),
        ),
        compiler_params=pltpu.CompilerParams(vmem_limit_bytes=LIMIT),
        name="project",
    )(frames, weights, grad, chunk)


def near_tiles(place, u):
    shift = place[1] - u
    first = jnp.where(shift >= 0, -2, -1)
    return [(place[0] + first + w, G * (first + w) + shift) for w in range(4)]


def band_at(apart):
    return pl.ds(pl.multiple_of((apart + REACH) * B, B), 2 * B)


def block_at(v):
    return pl.ds(pl.multiple_of((v + SPAN) * B, B), B)


def stats_kernel(
    place,
    mine_ref,
    theirs_ref,
    far_ref,
    weight_ref,
    slope_ref,
    near_ref,
    stats_ref,
    tops_ref,
    table_ref,
    shifts,
    content_ref,
):
    clip = place[2]
    table_ref[:, :PAD] = jnp.zeros((E, PAD), BF)
    table_ref[:, WIDE - PAD :] = jnp.zeros((E, PAD), BF)
    first = place[1] % 2 == 0
    def sides(k, rows):
        mine = mine_ref[k, rows].astype(F32)
        theirs = theirs_ref[k, rows].astype(F32)
        return jnp.where(first, mine, theirs), jnp.where(first, theirs, mine)

    for k in range(PAIRS):
        left, right = sides(k, slice(0, B))
        near_ref[2 * k] = left.astype(BF)
        near_ref[2 * k + 1] = right.astype(BF)
        for y in range(G):
            left, right = sides(k, slice(B + CHUNK * y, B + CHUNK * (y + 1)))
            top = jnp.concatenate([left[:, :E], right[:, :E]], axis=1)
            end = jnp.concatenate([left[:, E:], right[:, E:]], axis=1)
            at = PAD + (4 * y + k) * B
            table_ref[:, at : at + B] = jnp.concatenate([top, end], axis=0).astype(BF)
    offsets = lax.broadcasted_iota(jnp.int32, (E, WIDE), 1) - (TABLE // 2 + PAD)
    rows = table_ref[...].astype(F32)
    upper = jnp.sum(jnp.where(offsets == clip, rows, 0.0), axis=1, keepdims=True)
    lower = jnp.sum(jnp.where(offsets == -clip, rows, 0.0), axis=1, keepdims=True)
    rows = jnp.where(offsets >= clip, upper, jnp.where(offsets <= -clip, lower, rows))
    table_ref[...] = rows.astype(BF)

    keys = far_ref[:, :B, :E].reshape(N, E)
    values = far_ref[:, :B, E:].reshape(N, E)
    ends = jnp.concatenate([table_ref[:, :B], table_ref[:, WIDE - B :]], axis=1)
    lane = lax.broadcasted_iota(jnp.int32, (B, B), 1)
    row = lax.broadcasted_iota(jnp.int32, (B, B), 0)
    late = lane + row < B

    def put_band(u, v, apart):
        band = nn(near_ref[u, :, :E], table_ref[:, band_at(apart)])
        picked = jnp.where(late, band[:, B:], band[:, :B])
        shifts[u, :, block_at(v)] = pltpu.roll(picked, 0, 1, stride=1, stride_axis=0)

    for u in range(G):
        edges = nn(near_ref[u, :, :E], ends)
        for v in range(G):
            at = (v + SPAN) * B
            shifts[u, :, at : at + B] = jnp.where(v > place[0], edges[:, B:], edges[:, :B])
    put_band(place[1], place[0] + 2, 2 * G)
    queries = near_ref[:, :, :E].reshape(N, E)
    grads = near_ref[:, :, E:].reshape(N, E)
    for at in range(0, N, 2 * B):
        content_ref[:, at : at + 2 * B] = nt(queries, keys[at : at + 2 * B])
        slope_ref[:, at : at + 2 * B] = nt(grads, values[at : at + 2 * B])
    for u in range(G):
        rows = slice(u * B, (u + 1) * B)
        for v, apart in near_tiles(place, u):
            put_band(u, v, apart)
        pieces = []
        for v in range(G):
            at = (v + SPAN) * B
            both = content_ref[rows, v * B : (v + 1) * B] + shifts[u, :, at : at + B]
            pieces.append(jnp.where(lane < place[3 + G * v + place[1]], both, HIDDEN))
        scores = jnp.concatenate(pieces, axis=1)
        top = jnp.max(scores, axis=1, keepdims=True)
        weight = jnp.exp(scores - top)
        weight_ref[rows, :] = weight
        amount = jnp.sum(weight, axis=1, keepdims=True)
        mean = jnp.sum(weight * slope_ref[rows, :], axis=1, keepdims=True) / amount
        both = jnp.where(lane == 0, top + jnp.log(amount), jnp.where(lane == 1, mean, top))
        turned = both.T
        stats_ref[u : u + 1, :] = turned[0:1]
        stats_ref[G + u : G + u + 1, :] = turned[1:2]
        tops_ref[u : u + 1, :] = turned[2:3]


def statistics(place, mine, theirs, far):
    return pl.pallas_call(
        stats_kernel,
        in_specs=[SCALARS] + [ARRAY] * 3,
        out_specs=[ARRAY] * 6,
        out_shape=(
            jax.ShapeDtypeStruct((N, N), F32),
            jax.ShapeDtypeStruct((N, N), F32),
            jax.ShapeDtypeStruct((G, B, B), BF),
            jax.ShapeDtypeStruct((2 * G, B), F32),
            jax.ShapeDtypeStruct((G, B), F32),
            jax.ShapeDtypeStruct((E, WIDE), BF),
        ),
        scratch_shapes=[pltpu.VMEM((G, B, N + 2 * SPAN * B), F32), pltpu.VMEM((N, N), F32)],
        compiler_params=pltpu.CompilerParams(vmem_limit_bytes=LIMIT),
        name="statistics",
    )(place, mine, theirs, far)


def grads_kernel(
    place,
    near_ref,
    far_ref,
    weight_ref,
    slope_ref,
    tops_ref,
    parts_ref,
    table_ref,
    far_out,
    keep_out,
    send_out,
    query_sum,
    table_sum,
    held,
    lows,
    probs,
    outers,
):
    clip = place[2]
    parts = parts_ref[...]
    each = parts[:, :G]
    top = jnp.max(each, axis=0)
    total = top + jnp.log(jnp.sum(jnp.exp(each - top[None]), axis=0))
    mean = jnp.sum(jnp.exp(each - total[None]) * parts[:, G:], axis=0)
    rest = jnp.zeros((B - 2 * G, B), F32)
    columns = jnp.concatenate([jnp.exp(tops_ref[...] - total), mean, rest], axis=0).T
    table_sum[...] = jnp.zeros_like(table_sum)
    held[:, :, : SPAN * B] = jnp.zeros((G, B, SPAN * B), F32)
    held[:, :, SPAN * B + N :] = jnp.zeros((G, B, SPAN * B), F32)

    keys = far_ref[:, :B, :E].reshape(N, E)
    low_end, high_end = table_ref[:, :B], table_ref[:, WIDE - B :]
    ends = jnp.concatenate([low_end, high_end, low_end, high_end], axis=1)
    row = lax.broadcasted_iota(jnp.int32, (B, B), 0)
    lane = lax.broadcasted_iota(jnp.int32, (B, B), 1)
    turn = (lane + row) % B
    early = lane + row < B
    turned = []

    def add_band(u, v, apart, flipped):
        spun = jnp.take_along_axis(held[u, :, block_at(v)], turn, axis=1)
        band = jnp.concatenate(
            [jnp.where(early, 0.0, spun), jnp.where(early, spun, 0.0)], axis=1
        ).astype(BF)
        table_sum[:, band_at(apart)] += nn(flipped[:E], band)
        return nt(band, table_ref[:, band_at(apart)])

    for u in range(G):
        paired = near_ref[u]
        flipped = paired.astype(F32).T.astype(BF)
        turned.append(flipped)
        factor = columns[:, u : u + 1]
        mean = columns[:, G + u : G + u + 1]
        rows = slice(u * B, (u + 1) * B)
        prob = weight_ref[rows, :] * factor
        low = (prob * (slope_ref[rows, :] - mean)).astype(BF)
        lows[rows, :] = low
        probs[rows, :] = prob.astype(BF)
        wide = low.astype(F32)
        held[u, :, SPAN * B : SPAN * B + N] = wide
        lower = jnp.zeros((B, B), F32)
        upper = jnp.zeros((B, B), F32)
        for v in range(G):
            apart = G * (v - place[0]) + place[1] - u
            piece = wide[:, v * B : (v + 1) * B]
            lower = lower + jnp.where(apart <= -REACH, piece, 0.0)
            upper = upper + jnp.where(apart >= REACH, piece, 0.0)
        outer = jnp.concatenate([lower, upper], axis=1)
        coarse = outer.astype(BF)
        fine = (outer - coarse.astype(F32)).astype(BF)
        outers[rows, :] = jnp.concatenate([coarse, fine], axis=1)
        query_sum[u] = sum(add_band(u, v, apart, flipped) for v, apart in near_tiles(place, u))
    flipped = near_ref[place[1]].astype(F32).T.astype(BF)
    query_sum[place[1]] += add_band(place[1], place[0] + 2, 2 * G, flipped)
    both = jnp.concatenate(turned, axis=1)
    main = nn(lows[...], keys) + nt(outers[...], ends)
    tails = nn(both[:E], outers[...])
    first = place[1] % 2 == 0

    def split(k, rows, left, right):
        keep_out[k, rows] = jnp.where(first, left, right)
        send_out[k, rows] = jnp.where(first, right, left).astype(BF)

    packed = []
    for u in range(G):
        query = (query_sum[u] + main[u * B : (u + 1) * B]) * SCALE
        packed.append(jnp.concatenate([query[:E], query[E:]], axis=1))
    for k in range(PAIRS):
        split(k, slice(0, E), packed[2 * k], packed[2 * k + 1])
    pairs = jnp.concatenate([nn(both[:E], lows[...]), nn(both[E:], probs[...])], axis=0)
    offsets = lax.broadcasted_iota(jnp.int32, (E, WIDE), 1) - (TABLE // 2 + PAD)
    terms = table_sum[...]
    tails = tails[:, : 2 * B] + tails[:, 2 * B :]
    upper = jnp.sum(jnp.where(offsets >= clip, terms, 0.0), axis=1, keepdims=True)
    lower = jnp.sum(jnp.where(offsets <= -clip, terms, 0.0), axis=1, keepdims=True)
    upper = upper + jnp.sum(tails[:, B:], axis=1, keepdims=True)
    lower = lower + jnp.sum(tails[:, :B], axis=1, keepdims=True)
    table_sum[...] = jnp.where(offsets == clip, upper, jnp.where(offsets == -clip, lower, terms))
    for k in range(PAIRS):
        for y in range(G):
            at = PAD + (4 * y + k) * B
            block = table_sum[:, at : at + B]
            block = jnp.where(jnp.abs(lane[:E] + (at - TABLE // 2 - PAD)) <= clip, block, 0.0)
            top, end = block[:CHUNK], block[CHUNK:]
            left = jnp.concatenate([top[:, :E], end[:, :E]], axis=1)
            right = jnp.concatenate([top[:, E:], end[:, E:]], axis=1)
            split(k, slice(E + CHUNK * y, E + CHUNK * (y + 1)), left, right)
    for y in range(G):
        far_out[y] = pairs[:, y * B : (y + 1) * B].T.astype(BF)


def gradients(place, near, far, weight, slope, tops, parts, table):
    return pl.pallas_call(
        grads_kernel,
        in_specs=[SCALARS] + [ARRAY] * 7,
        out_specs=[ARRAY] * 3,
        out_shape=(
            jax.ShapeDtypeStruct((G, B, B), BF),
            jax.ShapeDtypeStruct((PAIRS, BACK, B), F32),
            jax.ShapeDtypeStruct((PAIRS, BACK, B), BF),
        ),
        scratch_shapes=[
            pltpu.VMEM((G, B, E), F32),
            pltpu.VMEM((E, WIDE), F32),
            pltpu.VMEM((G, B, N + 2 * SPAN * B), F32),
            pltpu.VMEM((N, N), BF),
            pltpu.VMEM((N, N), BF),
            pltpu.VMEM((N, 4 * B), BF),
        ],
        compiler_params=pltpu.CompilerParams(vmem_limit_bytes=LIMIT),
        name="gradients",
    )(place, near, far, weight, slope, tops, parts, table)


def fold_kernel(near_ref, pairs_ref, query_ref, far_ref):
    total = jnp.sum(near_ref[...].astype(F32), axis=0).astype(BF)
    query_ref[...] = jnp.concatenate([total[:E, :E], total[:E, E:]], axis=0)
    for y in range(G):
        far_ref[y, B:] = total[E + CHUNK * y : E + CHUNK * (y + 1)]
    far_ref[:, :B] = pairs_ref[...]


def fold(near, pairs):
    return pl.pallas_call(
        fold_kernel,
        out_shape=(jax.ShapeDtypeStruct((B, E), BF), jax.ShapeDtypeStruct((G, ROWS, B), BF)),
        compiler_params=pltpu.CompilerParams(vmem_limit_bytes=LIMIT),
        name="fold",
    )(near, pairs)


def unproject_kernel(far_ref, query_ref, weights_ref, out_ref, table_ref):
    total = jnp.sum(far_ref[...].astype(F32), axis=0)
    pairs = total[:B].astype(BF)
    table_ref[...] = total[B:]
    terms = nn(query_ref[...], weights_ref[:E]) + nn(pairs, weights_ref[E:])
    for h in range(G):
        out_ref[h] = terms[:, h * B : (h + 1) * B].astype(BF)


def unproject(far, query, weights):
    return pl.pallas_call(
        unproject_kernel,
        out_shape=(
            jax.ShapeDtypeStruct((G, B, B), BF),
            jax.ShapeDtypeStruct((E // 2, B), F32),
        ),
        compiler_params=pltpu.CompilerParams(vmem_limit_bytes=LIMIT),
        name="unproject",
    )(far, query, weights)


def exchange(parts, axis):
    return lax.all_to_all(parts, axis, 0, 0, tiled=True)


def to_all(shard):
    return jnp.broadcast_to(shard[None], (G,) + shard.shape)


def other_core(shard):
    return lax.ppermute(shard, "core", [(0, 1), (1, 0)])


def shards(frames, weights, offset_table, clip_range, valid_frames, context_grad):
    weight_rows = weights.reshape(3 * E, G * B)
    own = jnp.stack([lax.axis_index("far"), lax.axis_index(("pair", "core")), clip_range[0]])
    place = jnp.concatenate([own, valid_frames])
    turned = offset_table.T
    chunk = jnp.concatenate([turned[: E // 2], turned[E // 2 :]], axis=1)
    gathered = exchange(to_all(frames), "head")
    near, far = project(gathered, weight_rows, context_grad, chunk)
    far = exchange(far, "far")
    chunks = jnp.broadcast_to(far[:, B:].reshape(1, 4 * E, B), (PAIRS, 4 * E, B))
    mine = exchange(near.at[:, B:].set(chunks), "pair")
    theirs = other_core(mine)
    weight, slope, near, stats, tops, table = statistics(place, mine, theirs, far)
    parts = exchange(to_all(stats), ("pair", "core"))
    pairs, keep, send = gradients(
        place, near, far, weight, slope, tops, parts, table
    )
    halves = (keep + other_core(send).astype(F32)).astype(BF)
    query, far = fold(exchange(halves, "pair"), pairs)
    terms, table_part = unproject(exchange(far, "far"), query, weight_rows)
    table_grad = table_part.reshape(E // 2, 2, E).transpose(2, 1, 0).reshape(E, E)
    terms = exchange(terms, "head")
    input_grad = jnp.sum(terms.astype(F32), axis=0).astype(BF)
    return (input_grad, table_grad)


def solution(mesh):
    split = Mesh(mesh.devices.reshape(G, PAIRS, 2, G), ("far", "pair", "core", "head"))
    seq = ("far", "pair", "core")
    placed = (
        P(seq, "head"),
        P(None, "head", None),
        P(seq, "head"),
        P("head"),
        P(),
        P(seq, "head"),
    )
    return jax.shard_map(
        shards,
        mesh=split,
        in_specs=placed,
        out_specs=(P(seq, "head"), P(seq, "head")),
        check_vma=False,
    )
```

```python
import jax
import jax.numpy as jnp
from jax import lax
from jax.experimental import pallas as pl
from jax.experimental.pallas import tpu as pltpu
from jax.sharding import Mesh
from jax.sharding import PartitionSpec as P

B = 128
G = 8
E = 64
N = B * G
TABLE = 4096
REACH = 17
PAD = 256
WIDE = TABLE + 2 * PAD
SCALE = E ** (-0.5)
SPAN = 2
PAIRS = 4
SHARE = B + 4 * E
BACK = E + 4 * E
CHUNK = E // 2
ROWS = B + E // 2
HIDDEN = -1e30
BF = jnp.bfloat16
F32 = jnp.float32
LIMIT = 32 * 1024 * 1024
SCALARS = pl.BlockSpec(memory_space=pltpu.SMEM)
ARRAY = pl.BlockSpec(memory_space=pltpu.VMEM)


def nt(a, b):
    return lax.dot_general(a, b, (((1,), (1,)), ((), ())), preferred_element_type=F32)


def nn(a, b):
    return lax.dot_general(a, b, (((1,), (0,)), ((), ())), preferred_element_type=F32)


def project_kernel(frames_ref, weights_ref, grad_ref, chunk_ref, near_ref, far_ref):
    total = jnp.zeros((B, 3 * E), F32)
    for h in range(G):
        total = total + nt(frames_ref[h], weights_ref[h])
    low = total.astype(BF)
    scaled = (low[:, :E].astype(F32) * SCALE).astype(BF)
    paired = jnp.concatenate([scaled, grad_ref[...]], axis=1)
    for g in range(PAIRS):
        near_ref[g, :B] = paired
        near_ref[g, B:] = jnp.zeros((4 * E, B), BF)
    for g in range(G):
        far_ref[g, :B] = low[:, E:]
        far_ref[g, B:] = chunk_ref[...]


def project(frames, weights, grad, chunk):
    return pl.pallas_call(
        project_kernel,
        out_shape=(
            jax.ShapeDtypeStruct((PAIRS, SHARE, B), BF),
            jax.ShapeDtypeStruct((G, ROWS, B), BF),
        ),
        compiler_params=pltpu.CompilerParams(vmem_limit_bytes=LIMIT),
        name="project",
    )(frames, weights, grad, chunk)


def near_tiles(place, u):
    shift = place[1] - u
    first = jnp.where(shift >= 0, -2, -1)
    return [(place[0] + first + w, G * (first + w) + shift) for w in range(4)]


def band_at(apart):
    return pl.ds(pl.multiple_of((apart + REACH) * B, B), 2 * B)


def block_at(v):
    return pl.ds(pl.multiple_of((v + SPAN) * B, B), B)


def stats_kernel(
    place,
    mine_ref,
    theirs_ref,
    far_ref,
    weight_ref,
    slope_ref,
    near_ref,
    stats_ref,
    tops_ref,
    table_ref,
    shifts,
    content_ref,
):
    clip = place[2]
    table_ref[:, :PAD] = jnp.zeros((E, PAD), BF)
    table_ref[:, WIDE - PAD :] = jnp.zeros((E, PAD), BF)
    first = place[1] % 2 == 0
    def sides(k, rows):
        mine = mine_ref[k, rows].astype(F32)
        theirs = theirs_ref[k, rows].astype(F32)
        return jnp.where(first, mine, theirs), jnp.where(first, theirs, mine)

    for k in range(PAIRS):
        left, right = sides(k, slice(0, B))
        near_ref[2 * k] = left.astype(BF)
        near_ref[2 * k + 1] = right.astype(BF)
        for y in range(G):
            left, right = sides(k, slice(B + CHUNK * y, B + CHUNK * (y + 1)))
            top = jnp.concatenate([left[:, :E], right[:, :E]], axis=1)
            end = jnp.concatenate([left[:, E:], right[:, E:]], axis=1)
            at = PAD + (4 * y + k) * B
            table_ref[:, at : at + B] = jnp.concatenate([top, end], axis=0).astype(BF)
    offsets = lax.broadcasted_iota(jnp.int32, (E, WIDE), 1) - (TABLE // 2 + PAD)
    rows = table_ref[...].astype(F32)
    upper = jnp.sum(jnp.where(offsets == clip, rows, 0.0), axis=1, keepdims=True)
    lower = jnp.sum(jnp.where(offsets == -clip, rows, 0.0), axis=1, keepdims=True)
    rows = jnp.where(offsets >= clip, upper, jnp.where(offsets <= -clip, lower, rows))
    table_ref[...] = rows.astype(BF)

    keys = far_ref[:, :B, :E].reshape(N, E)
    values = far_ref[:, :B, E:].reshape(N, E)
    ends = jnp.concatenate([table_ref[:, :B], table_ref[:, WIDE - B :]], axis=1)
    lane = lax.broadcasted_iota(jnp.int32, (B, B), 1)
    row = lax.broadcasted_iota(jnp.int32, (B, B), 0)
    late = lane + row < B

    def put_band(u, v, apart):
        band = nn(near_ref[u, :, :E], table_ref[:, band_at(apart)])
        picked = jnp.where(late, band[:, B:], band[:, :B])
        shifts[u, :, block_at(v)] = pltpu.roll(picked, 0, 1, stride=1, stride_axis=0)

    for u in range(G):
        edges = nn(near_ref[u, :, :E], ends)
        for v in range(G):
            at = (v + SPAN) * B
            shifts[u, :, at : at + B] = jnp.where(v > place[0], edges[:, B:], edges[:, :B])
    put_band(place[1], place[0] + 2, 2 * G)
    queries = near_ref[:, :, :E].reshape(N, E)
    grads = near_ref[:, :, E:].reshape(N, E)
    for at in range(0, N, 2 * B):
        content_ref[:, at : at + 2 * B] = nt(queries, keys[at : at + 2 * B])
        slope_ref[:, at : at + 2 * B] = nt(grads, values[at : at + 2 * B])
    for u in range(G):
        rows = slice(u * B, (u + 1) * B)
        for v, apart in near_tiles(place, u):
            put_band(u, v, apart)
        pieces = []
        for v in range(G):
            at = (v + SPAN) * B
            both = content_ref[rows, v * B : (v + 1) * B] + shifts[u, :, at : at + B]
            pieces.append(jnp.where(lane < place[3 + G * v + place[1]], both, HIDDEN))
        scores = jnp.concatenate(pieces, axis=1)
        top = jnp.max(scores, axis=1, keepdims=True)
        weight = jnp.exp(scores - top)
        weight_ref[rows, :] = weight
        amount = jnp.sum(weight, axis=1, keepdims=True)
        mean = jnp.sum(weight * slope_ref[rows, :], axis=1, keepdims=True) / amount
        both = jnp.where(lane == 0, top + jnp.log(amount), jnp.where(lane == 1, mean, top))
        turned = both.T
        stats_ref[u : u + 1, :] = turned[0:1]
        stats_ref[G + u : G + u + 1, :] = turned[1:2]
        tops_ref[u : u + 1, :] = turned[2:3]


def statistics(place, mine, theirs, far):
    return pl.pallas_call(
        stats_kernel,
        in_specs=[SCALARS] + [ARRAY] * 3,
        out_specs=[ARRAY] * 6,
        out_shape=(
            jax.ShapeDtypeStruct((N, N), F32),
            jax.ShapeDtypeStruct((N, N), F32),
            jax.ShapeDtypeStruct((G, B, B), BF),
            jax.ShapeDtypeStruct((2 * G, B), F32),
            jax.ShapeDtypeStruct((G, B), F32),
            jax.ShapeDtypeStruct((E, WIDE), BF),
        ),
        scratch_shapes=[pltpu.VMEM((G, B, N + 2 * SPAN * B), F32), pltpu.VMEM((N, N), F32)],
        compiler_params=pltpu.CompilerParams(vmem_limit_bytes=LIMIT),
        name="statistics",
    )(place, mine, theirs, far)


def grads_kernel(
    place,
    near_ref,
    far_ref,
    weight_ref,
    slope_ref,
    tops_ref,
    parts_ref,
    table_ref,
    far_out,
    keep_out,
    send_out,
    query_sum,
    table_sum,
    held,
    lows,
    probs,
    outers,
):
    clip = place[2]
    parts = parts_ref[...]
    each = parts[:, :G]
    top = jnp.max(each, axis=0)
    total = top + jnp.log(jnp.sum(jnp.exp(each - top[None]), axis=0))
    mean = jnp.sum(jnp.exp(each - total[None]) * parts[:, G:], axis=0)
    rest = jnp.zeros((B - 2 * G, B), F32)
    columns = jnp.concatenate([jnp.exp(tops_ref[...] - total), mean, rest], axis=0).T
    table_sum[...] = jnp.zeros_like(table_sum)
    held[:, :, : SPAN * B] = jnp.zeros((G, B, SPAN * B), F32)
    held[:, :, SPAN * B + N :] = jnp.zeros((G, B, SPAN * B), F32)

    keys = far_ref[:, :B, :E].reshape(N, E)
    low_end, high_end = table_ref[:, :B], table_ref[:, WIDE - B :]
    ends = jnp.concatenate([low_end, high_end, low_end, high_end], axis=1)
    row = lax.broadcasted_iota(jnp.int32, (B, B), 0)
    lane = lax.broadcasted_iota(jnp.int32, (B, B), 1)
    turn = (lane + row) % B
    early = lane + row < B
    turned = []

    def add_band(u, v, apart, flipped):
        spun = jnp.take_along_axis(held[u, :, block_at(v)], turn, axis=1)
        band = jnp.concatenate(
            [jnp.where(early, 0.0, spun), jnp.where(early, spun, 0.0)], axis=1
        ).astype(BF)
        table_sum[:, band_at(apart)] += nn(flipped[:E], band)
        return nt(band, table_ref[:, band_at(apart)])

    for u in range(G):
        paired = near_ref[u]
        flipped = paired.astype(F32).T.astype(BF)
        turned.append(flipped)
        factor = columns[:, u : u + 1]
        mean = columns[:, G + u : G + u + 1]
        rows = slice(u * B, (u + 1) * B)
        prob = weight_ref[rows, :] * factor
        low = (prob * (slope_ref[rows, :] - mean)).astype(BF)
        lows[rows, :] = low
        probs[rows, :] = prob.astype(BF)
        wide = low.astype(F32)
        held[u, :, SPAN * B : SPAN * B + N] = wide
        lower = jnp.zeros((B, B), F32)
        upper = jnp.zeros((B, B), F32)
        for v in range(G):
            apart = G * (v - place[0]) + place[1] - u
            piece = wide[:, v * B : (v + 1) * B]
            lower = lower + jnp.where(apart <= -REACH, piece, 0.0)
            upper = upper + jnp.where(apart >= REACH, piece, 0.0)
        outer = jnp.concatenate([lower, upper], axis=1)
        coarse = outer.astype(BF)
        fine = (outer - coarse.astype(F32)).astype(BF)
        outers[rows, :] = jnp.concatenate([coarse, fine], axis=1)
        query_sum[u] = sum(add_band(u, v, apart, flipped) for v, apart in near_tiles(place, u))
    flipped = near_ref[place[1]].astype(F32).T.astype(BF)
    query_sum[place[1]] += add_band(place[1], place[0] + 2, 2 * G, flipped)
    both = jnp.concatenate(turned, axis=1)
    main = nn(lows[...], keys) + nt(outers[...], ends)
    tails = nn(both[:E], outers[...])
    first = place[1] % 2 == 0

    def split(k, rows, left, right):
        keep_out[k, rows] = jnp.where(first, left, right)
        send_out[k, rows] = jnp.where(first, right, left).astype(BF)

    packed = []
    for u in range(G):
        query = (query_sum[u] + main[u * B : (u + 1) * B]) * SCALE
        packed.append(jnp.concatenate([query[:E], query[E:]], axis=1))
    for k in range(PAIRS):
        split(k, slice(0, E), packed[2 * k], packed[2 * k + 1])
    pairs = jnp.concatenate([nn(both[:E], lows[...]), nn(both[E:], probs[...])], axis=0)
    offsets = lax.broadcasted_iota(jnp.int32, (E, WIDE), 1) - (TABLE // 2 + PAD)
    terms = table_sum[...]
    tails = tails[:, : 2 * B] + tails[:, 2 * B :]
    upper = jnp.sum(jnp.where(offsets >= clip, terms, 0.0), axis=1, keepdims=True)
    lower = jnp.sum(jnp.where(offsets <= -clip, terms, 0.0), axis=1, keepdims=True)
    upper = upper + jnp.sum(tails[:, B:], axis=1, keepdims=True)
    lower = lower + jnp.sum(tails[:, :B], axis=1, keepdims=True)
    table_sum[...] = jnp.where(offsets == clip, upper, jnp.where(offsets == -clip, lower, terms))
    for k in range(PAIRS):
        for y in range(G):
            at = PAD + (4 * y + k) * B
            block = table_sum[:, at : at + B]
            block = jnp.where(jnp.abs(lane[:E] + (at - TABLE // 2 - PAD)) <= clip, block, 0.0)
            top, end = block[:CHUNK], block[CHUNK:]
            left = jnp.concatenate([top[:, :E], end[:, :E]], axis=1)
            right = jnp.concatenate([top[:, E:], end[:, E:]], axis=1)
            split(k, slice(E + CHUNK * y, E + CHUNK * (y + 1)), left, right)
    for y in range(G):
        far_out[y] = pairs[:, y * B : (y + 1) * B].T.astype(BF)


def gradients(place, near, far, weight, slope, tops, parts, table):
    return pl.pallas_call(
        grads_kernel,
        in_specs=[SCALARS] + [ARRAY] * 7,
        out_specs=[ARRAY] * 3,
        out_shape=(
            jax.ShapeDtypeStruct((G, B, B), BF),
            jax.ShapeDtypeStruct((PAIRS, BACK, B), F32),
            jax.ShapeDtypeStruct((PAIRS, BACK, B), BF),
        ),
        scratch_shapes=[
            pltpu.VMEM((G, B, E), F32),
            pltpu.VMEM((E, WIDE), F32),
            pltpu.VMEM((G, B, N + 2 * SPAN * B), F32),
            pltpu.VMEM((N, N), BF),
            pltpu.VMEM((N, N), BF),
            pltpu.VMEM((N, 4 * B), BF),
        ],
        compiler_params=pltpu.CompilerParams(vmem_limit_bytes=LIMIT),
        name="gradients",
    )(place, near, far, weight, slope, tops, parts, table)


def fold_kernel(near_ref, pairs_ref, query_ref, far_ref):
    total = jnp.sum(near_ref[...].astype(F32), axis=0).astype(BF)
    query_ref[...] = jnp.concatenate([total[:E, :E], total[:E, E:]], axis=0)
    for y in range(G):
        far_ref[y, B:] = total[E + CHUNK * y : E + CHUNK * (y + 1)]
    far_ref[:, :B] = pairs_ref[...]


def fold(near, pairs):
    return pl.pallas_call(
        fold_kernel,
        out_shape=(jax.ShapeDtypeStruct((B, E), BF), jax.ShapeDtypeStruct((G, ROWS, B), BF)),
        compiler_params=pltpu.CompilerParams(vmem_limit_bytes=LIMIT),
        name="fold",
    )(near, pairs)


def unproject_kernel(far_ref, query_ref, weights_ref, out_ref, table_ref):
    total = jnp.sum(far_ref[...].astype(F32), axis=0)
    pairs = total[:B].astype(BF)
    table_ref[...] = jnp.concatenate([total[B:, :E], total[B:, E:]], axis=0)
    terms = nn(query_ref[...], weights_ref[:E]) + nn(pairs, weights_ref[E:])
    for h in range(G):
        out_ref[h] = terms[:, h * B : (h + 1) * B].astype(BF)


def unproject(far, query, weights):
    return pl.pallas_call(
        unproject_kernel,
        out_shape=(
            jax.ShapeDtypeStruct((G, B, B), BF),
            jax.ShapeDtypeStruct((E, E), F32),
        ),
        compiler_params=pltpu.CompilerParams(vmem_limit_bytes=LIMIT),
        name="unproject",
    )(far, query, weights)


def exchange(parts, axis):
    return lax.all_to_all(parts, axis, 0, 0, tiled=True)


def to_all(shard):
    return jnp.broadcast_to(shard[None], (G,) + shard.shape)


def other_core(shard):
    return lax.ppermute(shard, "core", [(0, 1), (1, 0)])


def shards(frames, weights, offset_table, clip_range, valid_frames, context_grad):
    weight_rows = weights.reshape(3 * E, G * B)
    by_slice = weight_rows.reshape(3 * E, G, B).transpose(1, 0, 2)
    own = jnp.stack([lax.axis_index("far"), lax.axis_index(("pair", "core")), clip_range[0]])
    place = jnp.concatenate([own, valid_frames])
    turned = offset_table.T
    chunk = jnp.concatenate([turned[: E // 2], turned[E // 2 :]], axis=1)
    gathered = exchange(to_all(frames), "head")
    near, far = project(gathered, by_slice, context_grad, chunk)
    far = exchange(far, "far")
    chunks = jnp.broadcast_to(far[:, B:].reshape(1, 4 * E, B), (PAIRS, 4 * E, B))
    mine = exchange(near.at[:, B:].set(chunks), "pair")
    theirs = other_core(mine)
    weight, slope, near, stats, tops, table = statistics(place, mine, theirs, far)
    parts = exchange(to_all(stats), ("pair", "core"))
    pairs, keep, send = gradients(
        place, near, far, weight, slope, tops, parts, table
    )
    halves = (keep + other_core(send).astype(F32)).astype(BF)
    query, far = fold(exchange(halves, "pair"), pairs)
    terms, table_part = unproject(exchange(far, "far"), query, weight_rows)
    terms = exchange(terms, "head")
    input_grad = jnp.sum(terms.astype(F32), axis=0).astype(BF)
    return (input_grad, table_part.T)


def solution(mesh):
    split = Mesh(mesh.devices.reshape(G, PAIRS, 2, G), ("far", "pair", "core", "head"))
    seq = ("far", "pair", "core")
    placed = (
        P(seq, "head"),
        P(None, "head", None),
        P(seq, "head"),
        P("head"),
        P(),
        P(seq, "head"),
    )
    return jax.shard_map(
        shards,
        mesh=split,
        in_specs=placed,
        out_specs=(P(seq, "head"), P(seq, "head")),
        check_vma=False,
    )
```

```python
import jax
import jax.numpy as jnp
from jax import lax
from jax.experimental import pallas as pl
from jax.experimental.pallas import tpu as pltpu
from jax.sharding import Mesh
from jax.sharding import PartitionSpec as P

B = 128
G = 8
E = 64
N = B * G
TABLE = 4096
REACH = 17
PAD = 256
WIDE = TABLE + 2 * PAD
SCALE = E ** (-0.5)
SPAN = 2
PAIRS = 4
SHARE = B + 4 * E
BACK = E + 4 * E
CHUNK = E // 2
ROWS = B + E // 2
HIDDEN = -1e30
BF = jnp.bfloat16
F32 = jnp.float32
LIMIT = 32 * 1024 * 1024
SCALARS = pl.BlockSpec(memory_space=pltpu.SMEM)
ARRAY = pl.BlockSpec(memory_space=pltpu.VMEM)


def nt(a, b):
    return lax.dot_general(a, b, (((1,), (1,)), ((), ())), preferred_element_type=F32)


def nn(a, b):
    return lax.dot_general(a, b, (((1,), (0,)), ((), ())), preferred_element_type=F32)


def project_kernel(frames_ref, weights_ref, grad_ref, chunk_ref, near_ref, far_ref):
    total = jnp.zeros((B, 3 * E), F32)
    for h in range(G):
        total = total + nt(frames_ref[h], weights_ref[h])
    low = total.astype(BF)
    scaled = (low[:, :E].astype(F32) * SCALE).astype(BF)
    paired = jnp.concatenate([scaled, grad_ref[...]], axis=1)
    for g in range(PAIRS):
        near_ref[g, :B] = paired
        near_ref[g, B:] = jnp.zeros((4 * E, B), BF)
    for g in range(G):
        far_ref[g, :B] = low[:, E:]
        far_ref[g, B:] = chunk_ref[...]


def project(frames, weights, grad, chunk):
    return pl.pallas_call(
        project_kernel,
        out_shape=(
            jax.ShapeDtypeStruct((PAIRS, SHARE, B), BF),
            jax.ShapeDtypeStruct((G, ROWS, B), BF),
        ),
        compiler_params=pltpu.CompilerParams(vmem_limit_bytes=LIMIT),
        name="project",
    )(frames, weights, grad, chunk)


def near_tiles(place, u):
    shift = place[1] - u
    first = jnp.where(shift >= 0, -2, -1)
    return [(place[0] + first + w, G * (first + w) + shift) for w in range(4)]


def band_at(apart):
    return pl.ds(pl.multiple_of((apart + REACH) * B, B), 2 * B)


def block_at(v):
    return pl.ds(pl.multiple_of((v + SPAN) * B, B), B)


def stats_kernel(
    place,
    mine_ref,
    theirs_ref,
    far_ref,
    weight_ref,
    slope_ref,
    near_ref,
    stats_ref,
    tops_ref,
    table_ref,
    shifts,
    content_ref,
):
    clip = place[2]
    table_ref[:, :PAD] = jnp.zeros((E, PAD), BF)
    table_ref[:, WIDE - PAD :] = jnp.zeros((E, PAD), BF)
    first = place[1] % 2 == 0
    def sides(k, rows):
        mine = mine_ref[k, rows].astype(F32)
        theirs = theirs_ref[k, rows].astype(F32)
        return jnp.where(first, mine, theirs), jnp.where(first, theirs, mine)

    for k in range(PAIRS):
        left, right = sides(k, slice(0, B))
        near_ref[2 * k] = left.astype(BF)
        near_ref[2 * k + 1] = right.astype(BF)
        for y in range(G):
            left, right = sides(k, slice(B + CHUNK * y, B + CHUNK * (y + 1)))
            top = jnp.concatenate([left[:, :E], right[:, :E]], axis=1)
            end = jnp.concatenate([left[:, E:], right[:, E:]], axis=1)
            at = PAD + (4 * y + k) * B
            table_ref[:, at : at + B] = jnp.concatenate([top, end], axis=0).astype(BF)
    offsets = lax.broadcasted_iota(jnp.int32, (E, WIDE), 1) - (TABLE // 2 + PAD)
    rows = table_ref[...].astype(F32)
    upper = jnp.sum(jnp.where(offsets == clip, rows, 0.0), axis=1, keepdims=True)
    lower = jnp.sum(jnp.where(offsets == -clip, rows, 0.0), axis=1, keepdims=True)
    rows = jnp.where(offsets >= clip, upper, jnp.where(offsets <= -clip, lower, rows))
    table_ref[...] = rows.astype(BF)

    keys = far_ref[:, :B, :E].reshape(N, E)
    values = far_ref[:, :B, E:].reshape(N, E)
    ends = jnp.concatenate([table_ref[:, :B], table_ref[:, WIDE - B :]], axis=1)
    lane = lax.broadcasted_iota(jnp.int32, (B, B), 1)
    row = lax.broadcasted_iota(jnp.int32, (B, B), 0)
    late = lane + row < B

    def put_band(u, v, apart):
        band = nn(near_ref[u, :, :E], table_ref[:, band_at(apart)])
        picked = jnp.where(late, band[:, B:], band[:, :B])
        shifts[u, :, block_at(v)] = pltpu.roll(picked, 0, 1, stride=1, stride_axis=0)

    for u in range(G):
        edges = nn(near_ref[u, :, :E], ends)
        for v in range(G):
            at = (v + SPAN) * B
            shifts[u, :, at : at + B] = jnp.where(v > place[0], edges[:, B:], edges[:, :B])
    put_band(place[1], place[0] + 2, 2 * G)
    for u in range(G):
        for v, apart in near_tiles(place, u):
            put_band(u, v, apart)
    queries = near_ref[:, :, :E].reshape(N, E)
    grads = near_ref[:, :, E:].reshape(N, E)
    for at in range(0, N, 2 * B):
        content_ref[:, at : at + 2 * B] = nt(queries, keys[at : at + 2 * B])
        slope_ref[:, at : at + 2 * B] = nt(grads, values[at : at + 2 * B])
    for u in range(G):
        rows = slice(u * B, (u + 1) * B)
        pieces = []
        for v in range(G):
            at = (v + SPAN) * B
            both = content_ref[rows, v * B : (v + 1) * B] + shifts[u, :, at : at + B]
            pieces.append(jnp.where(lane < place[3 + G * v + place[1]], both, HIDDEN))
        scores = jnp.concatenate(pieces, axis=1)
        top = jnp.max(scores, axis=1, keepdims=True)
        weight = jnp.exp(scores - top)
        weight_ref[rows, :] = weight
        amount = jnp.sum(weight, axis=1, keepdims=True)
        mean = jnp.sum(weight * slope_ref[rows, :], axis=1, keepdims=True) / amount
        both = jnp.where(lane == 0, top + jnp.log(amount), jnp.where(lane == 1, mean, top))
        turned = both.T
        stats_ref[u : u + 1, :] = turned[0:1]
        stats_ref[G + u : G + u + 1, :] = turned[1:2]
        tops_ref[u : u + 1, :] = turned[2:3]


def statistics(place, mine, theirs, far):
    return pl.pallas_call(
        stats_kernel,
        in_specs=[SCALARS] + [ARRAY] * 3,
        out_specs=[ARRAY] * 6,
        out_shape=(
            jax.ShapeDtypeStruct((N, N), F32),
            jax.ShapeDtypeStruct((N, N), F32),
            jax.ShapeDtypeStruct((G, B, B), BF),
            jax.ShapeDtypeStruct((2 * G, B), F32),
            jax.ShapeDtypeStruct((G, B), F32),
            jax.ShapeDtypeStruct((E, WIDE), BF),
        ),
        scratch_shapes=[pltpu.VMEM((G, B, N + 2 * SPAN * B), F32), pltpu.VMEM((N, N), F32)],
        compiler_params=pltpu.CompilerParams(vmem_limit_bytes=LIMIT),
        name="statistics",
    )(place, mine, theirs, far)


def grads_kernel(
    place,
    near_ref,
    far_ref,
    weight_ref,
    slope_ref,
    tops_ref,
    parts_ref,
    table_ref,
    far_out,
    keep_out,
    send_out,
    query_sum,
    table_sum,
    held,
    lows,
    probs,
    outers,
):
    clip = place[2]
    parts = parts_ref[...]
    each = parts[:, :G]
    top = jnp.max(each, axis=0)
    total = top + jnp.log(jnp.sum(jnp.exp(each - top[None]), axis=0))
    mean = jnp.sum(jnp.exp(each - total[None]) * parts[:, G:], axis=0)
    rest = jnp.zeros((B - 2 * G, B), F32)
    columns = jnp.concatenate([jnp.exp(tops_ref[...] - total), mean, rest], axis=0).T
    table_sum[...] = jnp.zeros_like(table_sum)
    held[:, :, : SPAN * B] = jnp.zeros((G, B, SPAN * B), F32)
    held[:, :, SPAN * B + N :] = jnp.zeros((G, B, SPAN * B), F32)

    keys = far_ref[:, :B, :E].reshape(N, E)
    low_end, high_end = table_ref[:, :B], table_ref[:, WIDE - B :]
    ends = jnp.concatenate([low_end, high_end, low_end, high_end], axis=1)
    row = lax.broadcasted_iota(jnp.int32, (B, B), 0)
    lane = lax.broadcasted_iota(jnp.int32, (B, B), 1)
    turn = (lane + row) % B
    early = lane + row < B
    turned = []

    def add_band(u, v, apart, flipped):
        spun = jnp.take_along_axis(held[u, :, block_at(v)], turn, axis=1)
        band = jnp.concatenate(
            [jnp.where(early, 0.0, spun), jnp.where(early, spun, 0.0)], axis=1
        ).astype(BF)
        table_sum[:, band_at(apart)] += nn(flipped[:E], band)
        return nt(band, table_ref[:, band_at(apart)])

    for u in range(G):
        paired = near_ref[u]
        flipped = paired.astype(F32).T.astype(BF)
        turned.append(flipped)
        factor = columns[:, u : u + 1]
        mean = columns[:, G + u : G + u + 1]
        rows = slice(u * B, (u + 1) * B)
        prob = weight_ref[rows, :] * factor
        low = (prob * (slope_ref[rows, :] - mean)).astype(BF)
        lows[rows, :] = low
        probs[rows, :] = prob.astype(BF)
        wide = low.astype(F32)
        held[u, :, SPAN * B : SPAN * B + N] = wide
        lower = jnp.zeros((B, B), F32)
        upper = jnp.zeros((B, B), F32)
        for v in range(G):
            apart = G * (v - place[0]) + place[1] - u
            piece = wide[:, v * B : (v + 1) * B]
            lower = lower + jnp.where(apart <= -REACH, piece, 0.0)
            upper = upper + jnp.where(apart >= REACH, piece, 0.0)
        outer = jnp.concatenate([lower, upper], axis=1)
        coarse = outer.astype(BF)
        fine = (outer - coarse.astype(F32)).astype(BF)
        outers[rows, :] = jnp.concatenate([coarse, fine], axis=1)
        query_sum[u] = sum(add_band(u, v, apart, flipped) for v, apart in near_tiles(place, u))
    flipped = near_ref[place[1]].astype(F32).T.astype(BF)
    query_sum[place[1]] += add_band(place[1], place[0] + 2, 2 * G, flipped)
    both = jnp.concatenate(turned, axis=1)
    main = nn(lows[...], keys) + nt(outers[...], ends)
    tails = nn(both[:E], outers[...])
    first = place[1] % 2 == 0

    def split(k, rows, left, right):
        keep_out[k, rows] = jnp.where(first, left, right)
        send_out[k, rows] = jnp.where(first, right, left).astype(BF)

    packed = []
    for u in range(G):
        query = (query_sum[u] + main[u * B : (u + 1) * B]) * SCALE
        packed.append(jnp.concatenate([query[:E], query[E:]], axis=1))
    for k in range(PAIRS):
        split(k, slice(0, E), packed[2 * k], packed[2 * k + 1])
    pairs = jnp.concatenate([nn(both[:E], lows[...]), nn(both[E:], probs[...])], axis=0)
    offsets = lax.broadcasted_iota(jnp.int32, (E, WIDE), 1) - (TABLE // 2 + PAD)
    terms = table_sum[...]
    tails = tails[:, : 2 * B] + tails[:, 2 * B :]
    upper = jnp.sum(jnp.where(offsets >= clip, terms, 0.0), axis=1, keepdims=True)
    lower = jnp.sum(jnp.where(offsets <= -clip, terms, 0.0), axis=1, keepdims=True)
    upper = upper + jnp.sum(tails[:, B:], axis=1, keepdims=True)
    lower = lower + jnp.sum(tails[:, :B], axis=1, keepdims=True)
    table_sum[...] = jnp.where(offsets == clip, upper, jnp.where(offsets == -clip, lower, terms))
    for k in range(PAIRS):
        for y in range(G):
            at = PAD + (4 * y + k) * B
            block = table_sum[:, at : at + B]
            block = jnp.where(jnp.abs(lane[:E] + (at - TABLE // 2 - PAD)) <= clip, block, 0.0)
            top, end = block[:CHUNK], block[CHUNK:]
            left = jnp.concatenate([top[:, :E], end[:, :E]], axis=1)
            right = jnp.concatenate([top[:, E:], end[:, E:]], axis=1)
            split(k, slice(E + CHUNK * y, E + CHUNK * (y + 1)), left, right)
    for y in range(G):
        far_out[y] = pairs[:, y * B : (y + 1) * B].T.astype(BF)


def gradients(place, near, far, weight, slope, tops, parts, table):
    return pl.pallas_call(
        grads_kernel,
        in_specs=[SCALARS] + [ARRAY] * 7,
        out_specs=[ARRAY] * 3,
        out_shape=(
            jax.ShapeDtypeStruct((G, B, B), BF),
            jax.ShapeDtypeStruct((PAIRS, BACK, B), F32),
            jax.ShapeDtypeStruct((PAIRS, BACK, B), BF),
        ),
        scratch_shapes=[
            pltpu.VMEM((G, B, E), F32),
            pltpu.VMEM((E, WIDE), F32),
            pltpu.VMEM((G, B, N + 2 * SPAN * B), F32),
            pltpu.VMEM((N, N), BF),
            pltpu.VMEM((N, N), BF),
            pltpu.VMEM((N, 4 * B), BF),
        ],
        compiler_params=pltpu.CompilerParams(vmem_limit_bytes=LIMIT),
        name="gradients",
    )(place, near, far, weight, slope, tops, parts, table)


def fold_kernel(near_ref, pairs_ref, query_ref, far_ref):
    total = jnp.sum(near_ref[...].astype(F32), axis=0).astype(BF)
    query_ref[...] = jnp.concatenate([total[:E, :E], total[:E, E:]], axis=0)
    for y in range(G):
        far_ref[y, B:] = total[E + CHUNK * y : E + CHUNK * (y + 1)]
    far_ref[:, :B] = pairs_ref[...]


def fold(near, pairs):
    return pl.pallas_call(
        fold_kernel,
        out_shape=(jax.ShapeDtypeStruct((B, E), BF), jax.ShapeDtypeStruct((G, ROWS, B), BF)),
        compiler_params=pltpu.CompilerParams(vmem_limit_bytes=LIMIT),
        name="fold",
    )(near, pairs)


def unproject_kernel(far_ref, query_ref, weights_ref, out_ref, table_ref):
    total = jnp.sum(far_ref[...].astype(F32), axis=0)
    pairs = total[:B].astype(BF)
    table_ref[...] = jnp.concatenate([total[B:, :E], total[B:, E:]], axis=0)
    terms = nn(jnp.concatenate([query_ref[...], pairs], axis=1), weights_ref[...])
    for h in range(G):
        out_ref[h] = terms[:, h * B : (h + 1) * B].astype(BF)


def unproject(far, query, weights):
    return pl.pallas_call(
        unproject_kernel,
        out_shape=(
            jax.ShapeDtypeStruct((G, B, B), BF),
            jax.ShapeDtypeStruct((E, E), F32),
        ),
        compiler_params=pltpu.CompilerParams(vmem_limit_bytes=LIMIT),
        name="unproject",
    )(far, query, weights)


def exchange(parts, axis):
    return lax.all_to_all(parts, axis, 0, 0, tiled=True)


def to_all(shard):
    return jnp.broadcast_to(shard[None], (G,) + shard.shape)


def other_core(shard):
    return lax.ppermute(shard, "core", [(0, 1), (1, 0)])


def shards(frames, weights, offset_table, clip_range, valid_frames, context_grad):
    weight_rows = weights.reshape(3 * E, G * B)
    by_slice = weight_rows.reshape(3 * E, G, B).transpose(1, 0, 2)
    own = jnp.stack([lax.axis_index("far"), lax.axis_index(("pair", "core")), clip_range[0]])
    place = jnp.concatenate([own, valid_frames])
    turned = offset_table.T
    chunk = jnp.concatenate([turned[: E // 2], turned[E // 2 :]], axis=1)
    gathered = exchange(to_all(frames), "head")
    near, far = project(gathered, by_slice, context_grad, chunk)
    far = exchange(far, "far")
    chunks = jnp.broadcast_to(far[:, B:].reshape(1, 4 * E, B), (PAIRS, 4 * E, B))
    mine = exchange(near.at[:, B:].set(chunks), "pair")
    theirs = other_core(mine)
    weight, slope, near, stats, tops, table = statistics(place, mine, theirs, far)
    parts = exchange(to_all(stats), ("pair", "core"))
    pairs, keep, send = gradients(
        place, near, far, weight, slope, tops, parts, table
    )
    halves = (keep + other_core(send).astype(F32)).astype(BF)
    query, far = fold(exchange(halves, "pair"), pairs)
    terms, table_part = unproject(exchange(far, "far"), query, weight_rows)
    terms = exchange(terms, "head")
    input_grad = jnp.sum(terms.astype(F32), axis=0).astype(BF)
    return (input_grad, table_part.T)


def solution(mesh):
    split = Mesh(mesh.devices.reshape(G, PAIRS, 2, G), ("far", "pair", "core", "head"))
    seq = ("far", "pair", "core")
    placed = (
        P(seq, "head"),
        P(None, "head", None),
        P(seq, "head"),
        P("head"),
        P(),
        P(seq, "head"),
    )
    return jax.shard_map(
        shards,
        mesh=split,
        in_specs=placed,
        out_specs=(P(seq, "head"), P(seq, "head")),
        check_vma=False,
    )
```
